512 devices in a mesh: frame: 16 (over z, core), head: 8 (over x, y_lo), dp: 4 (over y_hi).
Axes of the slice: x: 4, y: 8 (y_hi: 4, y_lo: 2; y = y_hi * 2 + y_lo), z: 8, core: 2. Of those that a mesh axis runs over, the one named last changes fastest.
Arguments:
- latents: bfloat16 [64, 512, 1152], P(('dp', 'frame'), None, 'head'), parts along dimension 0, may hold values from -36 to 36
- modulation: float32 [36, 1152], P('dp'), parts along dimension 0, may hold values from -3 to 3
- spatial_qkv: bfloat16 [1152, 3, 1152], P('frame', None, 'head'), may hold values from -1 to 1
- spatial_out: bfloat16 [1152, 1152], P('head', 'frame'), may hold values from -0.25 to 0.25
- temporal_qkv: bfloat16 [1152, 3, 1152], P('frame', None, 'head'), may hold values from -0.1875 to 0.1875
- temporal_out: bfloat16 [1152, 1152], P('head', 'frame'), may hold values from -0.25 to 0.25
- mlp_up: bfloat16 [1152, 4608], P('frame', 'head'), may hold values from -0.1875 to 0.1875
- mlp_down: bfloat16 [4608, 1152], P('head', 'frame'), may hold values from -0.125 to 0.125
Outputs:
- block_out: bfloat16 [64, 512, 1152], P(('dp', 'frame'), None, 'head'), parts along dimension 0
The draws below stay inside these ranges and needn't reach their ends.
There are 4 independent parts, one for each index of `dp`. The reference program is written for one: setup_inputs(seed, part) draws one part's arguments, and reference() takes and returns one part's arrays. A program takes and returns all parts, laid end to end along the dimension named above; an argument that names none is the same for every part. Nothing has to cross between parts.
All inputs are finite; a program needn't handle non-finite values.
Results may differ from the reference program's by a relative error of at most 0.023.
Values may be sent and summed in bfloat16 or wider, within the bound.
No kernel may reach another device: no remote copies, remote signals or barrier semaphores. Data moves between devices by JAX's collectives and lax.ppermute only.
A program may use at most 64 MiB of HBM per device.

```python
import math
import jax
import jax.numpy as jnp
from jax import lax

D = 1152
HEADS = 16
FF = 4608
PATCHES = 512
HEAD_DIM = 72
FRAMES = 16
GROUPS = 8


def draw_latents(key, part):
    key = jax.random.fold_in(key, 11)
    base_key, column_key, row_key = jax.random.split(key, 3)
    columns = jnp.exp(jax.random.uniform(column_key, (D,), jnp.float32, math.log(0.3), math.log(3.0)))
    row_scales = jnp.exp(jax.random.uniform(row_key, (FRAMES, PATCHES, 1), jnp.float32, math.log(0.5), math.log(2.0)))
    base = jnp.clip(jax.random.normal(base_key, (FRAMES, PATCHES, D), jnp.float32), -6.0, 6.0)
    return (base * columns * row_scales).astype(jnp.bfloat16)


def draw_modulation(key, part):
    key = jax.random.fold_in(key, 17)
    rows_key, sign_key, size_key, shift_key = jax.random.split(key, 4)
    signs = jnp.where(jax.random.bernoulli(sign_key, 0.5, (2, D)), 1.0, -1.0).astype(jnp.float32)
    rows = jnp.clip(0.5 * jax.random.normal(rows_key, (9, D), jnp.float32), -1.5, 1.5)
    sizes = jax.random.uniform(size_key, (2, D), jnp.float32, 1.5, 3.0)
    shift_row = jnp.clip(0.1 * jax.random.normal(shift_key, (D,), jnp.float32), -0.3, 0.3)
    gates = signs * sizes
    rows = rows.at[0].set(shift_row)
    rows = rows.at[2].set(gates[0])
    rows = rows.at[5].set(gates[1])
    return rows.astype(jnp.float32)


def draw_spatial_qkv(key, part):
    key = jax.random.fold_in(key, 23)
    query_key, noise_key, value_key = jax.random.split(key, 3)
    query_part = jnp.clip(jax.random.normal(query_key, (D, D), jnp.float32), -4.0, 4.0)
    noise_part = jnp.clip(jax.random.normal(noise_key, (D, D), jnp.float32), -4.0, 4.0)
    value_part = jnp.clip(jax.random.normal(value_key, (D, D), jnp.float32), -4.0, 4.0)
    key_part = 0.6 * query_part + 0.8 * noise_part
    stacked = jnp.stack([query_part, key_part, value_part], axis=1)
    return (stacked * (1.0 / math.sqrt(D))).astype(jnp.bfloat16)


def with_spikes(drawn, own_key, source, target, parts, factor):
    def block_of(dim):
        return (jnp.arange(drawn.shape[dim]) // (drawn.shape[dim] // parts)).reshape((-1,) + (1,) * (drawn.ndim - 1 - dim))

    near = jax.random.permutation(own_key, parts)[block_of(target)]
    far = (block_of(target) + parts // 2) % parts
    return jnp.where((block_of(source) == near) | (block_of(source) == far), factor * drawn, drawn)


def level_of(own_key, shape, pieces, smallest, largest):
    def one(axis_at, blocks):
        draws = jax.random.uniform(jax.random.fold_in(jax.random.fold_in(own_key, 6), axis_at), (blocks,), jnp.float32, smallest / len(pieces), largest / len(pieces))
        return jnp.repeat(jnp.exp(draws), shape[axis_at] // blocks).reshape((-1,) + (1,) * (len(shape) - axis_at - 1))

    level = one(*pieces[0])
    for cut in pieces[1:]:
        level = level * one(*cut)
    return level


def centred(own_key, dims, width, reach, shards=(), held_as=jnp.bfloat16):
    drawn = width * jax.random.normal(own_key, dims, jnp.float32)
    if shards:
        drawn = drawn * level_of(own_key, dims, shards, -0.22, 0.18)
    return jnp.clip(drawn, -reach, reach).astype(held_as)


def bell_draw_with(rng, shape, deviation, most, shards, heavy, held_as=jnp.bfloat16):
    entries = deviation * jax.random.normal(rng, shape, jnp.float32)
    if shards:
        entries = entries * level_of(rng, shape, shards, -0.22, 0.18)
    return jnp.clip(with_spikes(entries, jax.random.fold_in(rng, 3), *heavy), -most, most).astype(held_as)


def setup_inputs(seed: int = 0, part: int = 0) -> dict:
    seeds = jax.random.split(jax.random.key(seed), 9)
    own_keys = jax.random.split(jax.random.fold_in(seeds[8], part), 9)
    return {
        "latents": draw_latents(jax.random.fold_in(jax.random.fold_in(seeds[8], part), 71), part),
        "modulation": draw_modulation(jax.random.fold_in(jax.random.fold_in(seeds[8], part), 71), part),
        "spatial_qkv": draw_spatial_qkv(jax.random.fold_in(seeds[8], 71), part),
        "spatial_out": bell_draw_with(seeds[3], (D, D), D ** -0.5, 0.25, ((0, 8), (1, 16)), (0, 1, 16, 2.0)),
        "temporal_qkv": centred(seeds[4], (D, 3, D), D ** -0.5, 0.1875, ((0, 16), (2, 8))),
        "temporal_out": bell_draw_with(seeds[5], (D, D), D ** -0.5, 0.25, ((0, 8), (1, 16)), (0, 1, 16, 2.0)),
        "mlp_up": centred(seeds[6], (D, FF), D ** -0.5, 0.1875, ((0, 16), (1, 8))),
        "mlp_down": bell_draw_with(seeds[7], (FF, D), FF ** -0.5, 0.125, ((0, 8), (1, 16)), (0, 1, 16, 2.0)),
    }


norm_eps = 1e-06

def layer_mod(values, shift_row, scale_row):
    floats = values.astype(jnp.float32)
    center = floats - lax.optimization_barrier(jnp.mean(floats, axis=-1, keepdims=True))
    spread = lax.optimization_barrier(jnp.mean(center * center, axis=-1, keepdims=True))
    normal = center * lax.rsqrt(spread + norm_eps)
    return (normal * (1.0 + scale_row) + shift_row).astype(jnp.bfloat16)

def rms_scale(tensor):
    return tensor * lax.rsqrt(lax.optimization_barrier(jnp.mean(tensor * tensor, axis=-1, keepdims=True)) + norm_eps)

def split_heads(mixed_qkv):
    qkv_parts = mixed_qkv.reshape(mixed_qkv.shape[0], 3, HEADS, HEAD_DIM)
    query_rows = rms_scale(qkv_parts[:, 0]).astype(jnp.bfloat16)
    key_rows = rms_scale(qkv_parts[:, 1]).astype(jnp.bfloat16)
    value_rows = qkv_parts[:, 2].astype(jnp.bfloat16)
    return (query_rows, key_rows, value_rows)

def group_sum(values, weight):
    row_count, in_width = values.shape
    grouped = values.reshape(row_count, GROUPS, in_width // GROUPS).astype(jnp.float32)
    blocks = weight.reshape(GROUPS, in_width // GROUPS, weight.shape[1]).astype(jnp.float32)
    partial_value = jnp.einsum('rgc,gcd->grd', grouped, blocks, precision=lax.Precision.HIGHEST)
    rounded = lax.optimization_barrier(partial_value.astype(jnp.bfloat16))
    return lax.optimization_barrier(jnp.sum(rounded.astype(jnp.float32), axis=0))

def add_branch(stream, gate_row, summed):
    return (stream.astype(jnp.float32) + gate_row * summed).astype(jnp.bfloat16)

def reference(latents, modulation, spatial_qkv, spatial_out, temporal_qkv, temporal_out, mlp_up, mlp_down):
    factor = 1.0 / math.sqrt(HEAD_DIM)

    def spatial_frame(frame_rows):
        hidden = layer_mod(frame_rows, modulation[0], modulation[1])
        mixed_qkv = jnp.dot(hidden, spatial_qkv.reshape(D, 3 * D), preferred_element_type=jnp.float32)
        query_rows, key_rows, value_rows = split_heads(mixed_qkv)
        scores = jnp.einsum('qhd,khd->hqk', query_rows.astype(jnp.float32), key_rows.astype(jnp.float32)) * factor
        weights = jnp.exp(scores)
        weights = (weights / lax.optimization_barrier(jnp.sum(weights, axis=-1, keepdims=True))).astype(jnp.bfloat16)
        attended = jnp.einsum('hqk,khd->qhd', weights.astype(jnp.float32), value_rows.astype(jnp.float32))
        attended = attended.astype(jnp.bfloat16).reshape(PATCHES, D)
        return add_branch(frame_rows, modulation[2], group_sum(attended, spatial_out))
    first_stream = lax.map(spatial_frame, latents)
    hidden = layer_mod(first_stream, modulation[3], modulation[4]).reshape(FRAMES * PATCHES, D)
    mixed_qkv = jnp.dot(hidden, temporal_qkv.reshape(D, 3 * D), preferred_element_type=jnp.float32)
    query_rows, key_rows, value_rows = split_heads(mixed_qkv)
    query_rows = query_rows.reshape(FRAMES, PATCHES, HEADS, HEAD_DIM).astype(jnp.float32)
    key_rows = key_rows.reshape(FRAMES, PATCHES, HEADS, HEAD_DIM).astype(jnp.float32)
    value_rows = value_rows.reshape(FRAMES, PATCHES, HEADS, HEAD_DIM).astype(jnp.float32)
    scores = jnp.einsum('fphd,gphd->phfg', query_rows, key_rows) * factor
    weights = jnp.exp(scores)
    weights = (weights / lax.optimization_barrier(jnp.sum(weights, axis=-1, keepdims=True))).astype(jnp.bfloat16)
    attended = jnp.einsum('phfg,gphd->fphd', weights.astype(jnp.float32), value_rows)
    attended = attended.astype(jnp.bfloat16).reshape(FRAMES, PATCHES, D)

    def finish_frame(pair):
        frame_rows, attended_rows = pair
        second_stream = add_branch(frame_rows, modulation[5], group_sum(attended_rows, temporal_out))
        mlp_hidden = layer_mod(second_stream, modulation[6], modulation[7])
        raised = jnp.dot(mlp_hidden, mlp_up, preferred_element_type=jnp.float32)
        activation = jax.nn.gelu(raised, approximate=True).astype(jnp.bfloat16)
        return add_branch(second_stream, modulation[8], group_sum(activation, mlp_down))
    return lax.map(finish_frame, (first_stream, attended))
```

```python
import math

import jax
import jax.numpy as jnp
from jax import lax
from jax.sharding import PartitionSpec as P

HEAD_DIM = 72
EPS = 1e-06
FACTOR = 1.0 / math.sqrt(HEAD_DIM)


def norm_columns(values, shift, scale):
    center = values - jnp.mean(values, axis=0, keepdims=True)
    spread = jnp.mean(center * center, axis=0, keepdims=True)
    normal = center * lax.rsqrt(spread + EPS)
    return (normal * (1.0 + scale) + shift).astype(jnp.bfloat16)


def gather_head(block):
    count = lax.axis_size("head")
    copies = jnp.broadcast_to(block[None], (count,) + block.shape)
    return lax.all_to_all(copies, "head", 0, 0, tiled=True)


def swap_frames(block):
    count = lax.axis_size("frame")
    width, rows = block.shape
    inner = rows // count
    cut = block.reshape(width, count, inner).transpose(1, 0, 2).reshape(count, width * inner)
    moved = lax.all_to_all(cut, "frame", 0, 0, tiled=True)
    return moved.reshape(count, width, inner).transpose(1, 0, 2).reshape(width, rows)


def project(weight, hidden):
    return lax.dot_general(
        weight, hidden, (((0,), (0,)), ((), ())), preferred_element_type=jnp.float32
    )


def attention(mixed, mask):
    rows = mixed.shape[1]
    parts = mixed.reshape(3, -1, HEAD_DIM, rows)

    def rms(u):
        return (u * lax.rsqrt(jnp.mean(u * u, axis=1, keepdims=True) + EPS)).astype(jnp.bfloat16)

    query, key, value = rms(parts[0]), rms(parts[1]), parts[2].astype(jnp.bfloat16)
    scores = jnp.einsum("hdk,hdq->hkq", key, query, preferred_element_type=jnp.float32) * FACTOR
    weights = jnp.exp(scores)
    if mask is not None:
        weights = jnp.where(mask[None], weights, 0.0)
    weights = (weights / jnp.sum(weights, axis=1, keepdims=True)).astype(jnp.bfloat16)
    out = jnp.einsum("hdk,hkq->hdq", value, weights, preferred_element_type=jnp.float32)
    return out.astype(jnp.bfloat16).reshape(-1, rows)


def per_device(
    latents, modulation, spatial_qkv, spatial_out, temporal_qkv, temporal_out, mlp_up, mlp_down
):
    rows, width = latents.shape[1], latents.shape[2]
    heads_n, frames_n = lax.axis_size("head"), lax.axis_size("frame")
    full = width * heads_n
    place = rows // frames_n
    mine = lax.axis_index("head") * width
    depth = spatial_qkv.shape[0]
    mod = modulation.T
    col = lambda i: mod[:, i : i + 1]

    outs = jnp.stack([spatial_out.T, temporal_out.T])
    outs = gather_head(outs).transpose(1, 2, 0, 3).reshape(2, depth, full)
    t_qkv = temporal_qkv.reshape(depth, -1)
    pad = lambda a: jnp.pad(a, ((0, 0), (0, -a.shape[1] % 128)))
    pieces = [outs[0], outs[1], pad(t_qkv), pad(mlp_up), mlp_down.T]
    packed = lax.all_gather(jnp.concatenate(pieces, axis=1), "frame", axis=0, tiled=True)
    at, cuts = 0, []
    for piece, real in zip(pieces, (full, full, t_qkv.shape[1], mlp_up.shape[1], mlp_down.shape[0])):
        cuts.append(packed[:, at : at + real])
        at += piece.shape[1]
    s_out, t_out, t_qkv, w_up, w_down = cuts
    s_qkv = lax.all_gather(spatial_qkv.reshape(depth, -1), "frame", axis=0, tiled=True)

    own = latents.reshape(rows, width).T
    frame_latents = gather_head(own).reshape(full, rows).astype(jnp.float32)
    place_latents = gather_head(swap_frames(own)).reshape(full, rows)

    hidden = norm_columns(frame_latents, col(0), col(1))
    attended = attention(project(s_qkv, hidden), None)
    attended = gather_head(swap_frames(attended)).reshape(full, rows)

    branch = jnp.dot(s_out, attended, preferred_element_type=jnp.float32)
    stream = (place_latents.astype(jnp.float32) + col(2) * branch).astype(jnp.bfloat16)
    hidden = norm_columns(stream.astype(jnp.float32), col(3), col(4))
    spot = lax.broadcasted_iota(jnp.int32, (rows, rows), 0) % place
    spot_q = lax.broadcasted_iota(jnp.int32, (rows, rows), 1) % place
    attended = attention(project(t_qkv, hidden), spot == spot_q)
    attended = gather_head(attended).reshape(full, rows)

    branch = jnp.dot(t_out, attended, preferred_element_type=jnp.float32)
    stream = (stream.astype(jnp.float32) + col(5) * branch).astype(jnp.bfloat16)
    hidden = norm_columns(stream.astype(jnp.float32), col(6), col(7))
    active = jax.nn.gelu(project(w_up, hidden), approximate=True).astype(jnp.bfloat16)
    partial = jnp.dot(w_down, active, preferred_element_type=jnp.float32).astype(jnp.bfloat16)
    partial = lax.all_to_all(partial.reshape(heads_n, width, rows), "head", 0, 0, tiled=True)
    summed = jnp.sum(partial.astype(jnp.float32), axis=0)
    share = lax.dynamic_slice_in_dim(stream, mine, width, 0).astype(jnp.float32)
    gate = lax.dynamic_slice_in_dim(col(8), mine, width, 0)
    result = swap_frames((share + gate * summed).astype(jnp.bfloat16))
    return result.T.reshape(1, rows, width)


def solution(mesh):
    placed = (
        P(("dp", "frame"), None, "head"),
        P("dp", None),
        P("frame", None, "head"),
        P("head", "frame"),
        P("frame", None, "head"),
        P("head", "frame"),
        P("frame", "head"),
        P("head", "frame"),
    )
    return jax.shard_map(
        per_device,
        mesh=mesh,
        in_specs=placed,
        out_specs=P(("dp", "frame"), None, "head"),
        check_vma=False,
    )
```

```python
import math

import jax
import jax.numpy as jnp
from jax import lax
from jax.experimental import pallas as pl
from jax.experimental.pallas import tpu as pltpu
from jax.sharding import PartitionSpec as P

HEAD_DIM = 72
EPS = 1e-06
FACTOR = 1.0 / math.sqrt(HEAD_DIM)
LANES = 128
PLACE = 32
PARTS = LANES // PLACE
BLOCK = 144
FEATURES = 432


def project(weight, hidden):
    return lax.dot_general(
        weight, hidden, (((0,), (0,)), ((), ())), preferred_element_type=jnp.float32
    )


def lane_part(rows):
    return lax.broadcasted_iota(jnp.int32, (rows, LANES), 1) // PLACE


def pack(block, out_ref, group):
    features, rows = block.shape
    counts = [(at, min(group, features - at)) for at in range(0, features, group)]
    for tile in range(rows // LANES):
        cut = block[:, tile * LANES : (tile + 1) * LANES]
        for spot in range(PARTS):
            total = None
            for part, (at, count) in enumerate(counts):
                piece = cut[at : at + count]
                turn = (part - spot) * PLACE % LANES
                piece = pltpu.roll(piece, turn, 1) if turn else piece
                if count < group:
                    piece = jnp.concatenate([piece, jnp.zeros((group - count, LANES), piece.dtype)], 0)
                total = piece if total is None else jnp.where(lane_part(group) == part, piece, total)
            out_ref[tile * PARTS + spot] = total.astype(out_ref.dtype)


def unpack(in_ref, features, group):
    count = in_ref.shape[0]
    groups = [(at, min(group, features - at)) for at in range(0, features, group)]
    tiles = []
    for tile in range(count // PARTS):
        held = [in_ref[tile * PARTS + spot].astype(jnp.float32) for spot in range(PARTS)]
        pieces = []
        for part, (at, size) in enumerate(groups):
            total = None
            for spot in range(PARTS):
                turn = (spot - part) * PLACE % LANES
                piece = held[spot][:size]
                piece = pltpu.roll(piece, turn, 1) if turn else piece
                total = piece if total is None else jnp.where(lane_part(size) == spot, piece, total)
            pieces.append(total)
        tiles.append(jnp.concatenate(pieces, 0))
    return jnp.concatenate(tiles, 1)


def norm_heads(mixed):
    features, rows = mixed.shape
    parts = mixed.reshape(features // HEAD_DIM, HEAD_DIM, rows)
    scale = lax.rsqrt(jnp.mean(parts * parts, axis=1, keepdims=True) + EPS)
    normed = (parts * scale).reshape(features, rows)
    pairs = 2 * features // 3
    return jnp.concatenate([normed[:pairs], mixed[pairs:]], 0)


def attend(mixed, same=None):
    third = mixed.shape[0] // 3
    outs = []
    for at in range(0, third, HEAD_DIM):
        query, key, value = (mixed[at + i * third : at + i * third + HEAD_DIM] for i in range(3))
        weights = jnp.exp(project(key, query) * FACTOR)
        if same is not None:
            weights = jnp.where(same, weights, 0.0)
        weights = (weights / jnp.sum(weights, axis=0, keepdims=True)).astype(jnp.bfloat16)
        outs.append(jnp.dot(value, weights, preferred_element_type=jnp.float32))
    return jnp.concatenate(outs, 0)


def norm_rows(read, full, shift, scale, hidden_ref):
    steps = range(0, full, BLOCK)
    mean = sum(jnp.sum(read(at), axis=0, keepdims=True) for at in steps) / full
    spread = 0.0
    for at in steps:
        center = read(at) - mean
        spread += jnp.sum(center * center, axis=0, keepdims=True)
    inverse = lax.rsqrt(spread / full + EPS)
    for at in steps:
        spot = slice(at, at + BLOCK)
        normal = (read(at) - mean) * inverse
        hidden_ref[spot] = (normal * (1.0 + scale[spot]) + shift[spot]).astype(jnp.bfloat16)


def add_branch(weight, hidden, stream, gate, out_ref, whole_ref):
    for at in range(0, hidden.shape[0], BLOCK):
        spot = slice(at, at + BLOCK)
        branch = jnp.dot(weight(at), hidden, preferred_element_type=jnp.float32)
        total = (stream(at).astype(jnp.float32) + gate[spot] * branch).astype(jnp.bfloat16)
        out_ref[spot] = total
        whole_ref[spot] = total.astype(jnp.float32)


def weight_copies(weight_ref, held, sems, full, cuts):
    spots = [(pl.ds(at, BLOCK), pl.ds(0, full)) for at in range(0, full, BLOCK)]
    spots += [(pl.ds(0, full), pl.ds(at, count)) for at, count in cuts]
    copies = [
        pltpu.make_async_copy(weight_ref.at[spot], held.at[spot], sems.at[i])
        for i, spot in enumerate(spots)
    ]
    for copy in copies:
        copy.start()
    return copies


def turned_copies_kernel(in_ref, out_ref):
    turned = in_ref[...].T
    for at in range(out_ref.shape[0]):
        out_ref[at] = turned


def opening_kernel(own_ref, late_ref, mod_ref, rows_ref, mod_out_ref):
    rows, cols = own_ref.shape[1], late_ref.shape[1]
    for at in range(rows_ref.shape[0]):
        rows_ref[at, :, :rows] = own_ref[...]
        rows_ref[at, :, rows : rows + cols] = late_ref[...]
    mod_out_ref[...] = mod_ref[...].T


def spatial_kernel(
    rows_ref, weight_ref, mod_ref, up_ref, down_ref, out_ref, late_ref, hidden, up, down, sems
):
    full, rows = hidden.shape
    copies = [
        pltpu.make_async_copy(up_ref, up, sems.at[0]),
        pltpu.make_async_copy(down_ref, down, sems.at[1]),
    ]
    for copy in copies:
        copy.start()
    depth, units = up.shape
    late_ref[:, :full] = jnp.concatenate(
        [rows_ref[at, :, rows : rows + depth].T for at in range(rows_ref.shape[0])], 1
    )
    read = lambda at: rows_ref[at // BLOCK, :, :rows].astype(jnp.float32)
    norm_rows(read, full, mod_ref[:, 0:1], mod_ref[:, 1:2], hidden)
    mixed = norm_heads(project(weight_ref[...], hidden[...])).astype(jnp.bfloat16)
    block = attend(mixed).astype(out_ref.dtype)
    for at in range(out_ref.shape[0]):
        out_ref[at] = block
    for at, copy, held in zip((full, full + units + -units % LANES), copies, (up, down)):
        copy.wait()
        late_ref[:, at : at + units] = held[...]


def spatial_end_kernel(
    gathered_ref, rows_ref, weight_ref, mod_ref, mixed_ref, stream_ref, whole, hidden, held, sems
):
    full, rows = stream_ref.shape
    copies = weight_copies(weight_ref, held, sems, full, [(full, held.shape[1] - full)])

    def weight(at):
        copies[at // BLOCK].wait()
        return held[at : at + BLOCK, :full]

    add_branch(
        weight,
        gathered_ref[...].reshape(full, rows),
        lambda at: rows_ref[at // BLOCK, :, :rows],
        mod_ref[:, 2:3],
        stream_ref,
        whole,
    )
    norm_rows(lambda at: whole[at : at + BLOCK], full, mod_ref[:, 3:4], mod_ref[:, 4:5], hidden)
    copies[-1].wait()
    mixed = project(held[:, full : full + FEATURES], hidden[...])
    pack(norm_heads(mixed), mixed_ref, mixed_ref.shape[1])


def temporal_kernel(moved_ref, out_ref):
    mixed = unpack(moved_ref, FEATURES, moved_ref.shape[1]).astype(jnp.bfloat16)
    rows = mixed.shape[1]
    spot = lax.broadcasted_iota(jnp.int32, (rows, rows), 0) % PLACE
    spot_q = lax.broadcasted_iota(jnp.int32, (rows, rows), 1) % PLACE
    pack(attend(mixed, spot == spot_q), out_ref, out_ref.shape[1])


def copies_kernel(moved_ref, out_ref):
    block = unpack(moved_ref, out_ref.shape[1], moved_ref.shape[1]).astype(out_ref.dtype)
    for at in range(out_ref.shape[0]):
        out_ref[at] = block


def mlp_kernel(
    mine_ref, gathered_ref, before_ref, weight_ref, mod_ref, partial_ref, share_ref,
    stream, whole, hidden, active, held, sems,
):
    full, rows = stream.shape
    units = active.shape[0]
    down = full + units + -units % LANES
    cuts = [(full, down - full), (down, held.shape[1] - down)]
    copies = weight_copies(weight_ref, held, sems, full, cuts)

    def weight(at):
        copies[at // BLOCK].wait()
        return held[at : at + BLOCK, :full]

    add_branch(
        weight,
        gathered_ref[...].reshape(full, rows),
        lambda at: before_ref[at : at + BLOCK],
        mod_ref[:, 5:6],
        stream,
        whole,
    )
    share_ref[...] = whole[pl.ds(pl.multiple_of(mine_ref[0] * BLOCK, BLOCK), BLOCK), :]
    norm_rows(lambda at: whole[at : at + BLOCK], full, mod_ref[:, 6:7], mod_ref[:, 7:8], hidden)
    copies[-2].wait()
    raised = project(held[:, full : full + units], hidden[...])
    active[...] = jax.nn.gelu(raised, approximate=True).astype(jnp.bfloat16)
    copies[-1].wait()
    for at in range(0, full, BLOCK):
        lowered = jnp.dot(
            held[at : at + BLOCK, down : down + units], active[...], preferred_element_type=jnp.float32
        )
        partial_ref[at // BLOCK] = lowered.astype(jnp.bfloat16)


def closing_kernel(mine_ref, partial_ref, share_ref, mod_ref, out_ref):
    summed = jnp.sum(partial_ref[...].astype(jnp.float32), axis=0)
    gate = mod_ref[pl.ds(pl.multiple_of(mine_ref[0] * BLOCK, BLOCK), BLOCK), 8:9]
    out_ref[...] = (share_ref[...] + gate * summed).astype(out_ref.dtype)


HERE = pl.BlockSpec(memory_space=pltpu.VMEM)
THERE = pl.BlockSpec(memory_space=pltpu.HBM)
SCALAR = pl.BlockSpec(memory_space=pltpu.SMEM)


def vmem_call(kernel, out_shape, in_specs, scratch=(), limit=32):
    return pl.pallas_call(
        kernel,
        out_shape=out_shape,
        in_specs=in_specs,
        scratch_shapes=list(scratch),
        compiler_params=pltpu.CompilerParams(vmem_limit_bytes=limit * 2**20),
    )


def per_device(
    latents, modulation, spatial_qkv, spatial_out, temporal_qkv, temporal_out, mlp_up, mlp_down
):
    rows, width = latents.shape[1], latents.shape[2]
    heads_n, frames_n = lax.axis_size("head"), lax.axis_size("frame")
    full = width * heads_n
    depth = spatial_qkv.shape[0]
    units = mlp_up.shape[1]
    mine = lax.axis_index("head").astype(jnp.int32).reshape(1)
    array = lambda *shape, dtype=jnp.bfloat16: jax.ShapeDtypeStruct(shape, dtype)
    bf16 = lambda *shape: pltpu.VMEM(shape, jnp.bfloat16)
    f32 = lambda *shape: pltpu.VMEM(shape, jnp.float32)
    sems = lambda count: pltpu.SemaphoreType.DMA((count,))
    spread = lambda copies: lax.all_to_all(copies, "head", 0, 0, tiled=True)
    swap = lambda chunks: lax.all_to_all(chunks, "frame", 0, 0, tiled=True)
    pad = lambda a: jnp.pad(a, ((0, 0), (0, -a.shape[1] % LANES)))

    gather_frame = lambda packed: lax.all_gather(packed, "frame", axis=0, tiled=True)

    out_copies = vmem_call(turned_copies_kernel, array(heads_n, depth, width), [HERE])(spatial_out)
    row_copies, mod = vmem_call(
        opening_kernel,
        (
            array(heads_n, width, rows + LANES),
            array(full, modulation.shape[0], dtype=jnp.float32),
        ),
        [HERE] * 3,
    )(latents.reshape(rows, width).T, temporal_out, modulation)

    s_out = spread(out_copies).transpose(1, 0, 2).reshape(depth, full)
    early = gather_frame(
        jnp.concatenate([s_out, pad(temporal_qkv.reshape(depth, -1))], axis=1)
    )
    stream = spread(row_copies)
    s_qkv = gather_frame(spatial_qkv.reshape(depth, -1))

    attended, late = vmem_call(
        spatial_kernel,
        (array(heads_n, width, rows), array(depth, full + 2 * (units + -units % LANES))),
        [HERE] * 3 + [THERE] * 2,
        (bf16(full, rows), bf16(depth, units), bf16(depth, units), sems(2)),
    )(stream, s_qkv, mod, mlp_up, mlp_down.T)
    late = gather_frame(late)

    mixed, stream = vmem_call(
        spatial_end_kernel,
        (array(frames_n, 112, LANES), array(full, rows)),
        [HERE, HERE, THERE, HERE],
        (f32(full, rows), bf16(full, rows), bf16(*early.shape), sems(full // BLOCK + 1)),
        46,
    )(spread(attended), stream, early, mod)
    attended = vmem_call(temporal_kernel, array(frames_n, 48, LANES), [HERE])(swap(mixed))
    attended = vmem_call(copies_kernel, array(heads_n, width, rows), [HERE])(swap(attended))

    partial, share = vmem_call(
        mlp_kernel,
        (array(heads_n, width, rows), array(width, rows, dtype=jnp.float32)),
        [SCALAR, HERE, HERE, THERE, HERE],
        (
            bf16(full, rows), f32(full, rows), bf16(full, rows), bf16(units, rows),
            bf16(*late.shape), sems(full // BLOCK + 2),
        ),
        46,
    )(mine, spread(attended), stream, late, mod)
    result = vmem_call(closing_kernel, array(width, rows), [SCALAR, HERE, HERE, HERE])(
        mine, spread(partial), share, mod
    )
    return result.T.reshape(1, rows, width)


def solution(mesh):
    placed = (
        P(("dp", "frame"), None, "head"),
        P("dp", None),
        P("frame", None, "head"),
        P("head", "frame"),
        P("frame", None, "head"),
        P("head", "frame"),
        P("frame", "head"),
        P("head", "frame"),
    )
    return jax.shard_map(
        per_device,
        mesh=mesh,
        in_specs=placed,
        out_specs=P(("dp", "frame"), None, "head"),
        check_vma=False,
    )
```

```python
import math

import jax
import jax.numpy as jnp
from jax import lax
from jax.experimental import pallas as pl
from jax.experimental.pallas import tpu as pltpu
from jax.sharding import PartitionSpec as P

HEAD_DIM = 72
EPS = 1e-06
FACTOR = 1.0 / math.sqrt(HEAD_DIM)
LANES = 128
SHARES = 2
PLACE = 16
PARTS = LANES // PLACE
BLOCK = 144
FEATURES = 432


def project(weight, hidden):
    return lax.dot_general(
        weight, hidden, (((0,), (0,)), ((), ())), preferred_element_type=jnp.float32
    )


def exchange(pieces):
    part = lax.broadcasted_iota(jnp.int32, pieces[0].shape, 1) // PLACE
    step = 1
    while step < PARTS:
        held = list(pieces)
        high = (part // step) % 2 == 1
        for i in range(PARTS):
            if i & step:
                continue
            low_piece, high_piece = pieces[i], pieces[i + step]
            held[i] = jnp.where(high, pltpu.roll(high_piece, step * PLACE, 1), low_piece)
            held[i + step] = jnp.where(high, high_piece, pltpu.roll(low_piece, LANES - step * PLACE, 1))
        pieces, step = held, 2 * step
    return pieces


def pack(block, out_ref, group):
    features, rows = block.shape
    if features < PARTS * group:
        block = jnp.concatenate([block, jnp.zeros((PARTS * group - features, rows), block.dtype)], 0)
    for tile in range(rows // LANES):
        cut = block[:, tile * LANES : (tile + 1) * LANES]
        pieces = [cut[at : at + group] for at in range(0, PARTS * group, group)]
        for spot, piece in enumerate(exchange(pieces)):
            out_ref[tile * PARTS + spot] = piece.astype(out_ref.dtype)


def unpack(in_ref, features):
    tiles = []
    for tile in range(in_ref.shape[0] // PARTS):
        held = [in_ref[tile * PARTS + spot].astype(jnp.float32) for spot in range(PARTS)]
        tiles.append(jnp.concatenate(exchange(held), 0)[:features])
    return jnp.concatenate(tiles, 1)


def norm_heads(mixed):
    features, rows = mixed.shape
    parts = mixed.reshape(features // HEAD_DIM, HEAD_DIM, rows)
    scale = lax.rsqrt(jnp.mean(parts * parts, axis=1, keepdims=True) + EPS)
    normed = (parts * scale).reshape(features, rows)
    pairs = 2 * features // 3
    return jnp.concatenate([normed[:pairs], mixed[pairs:]], 0)


def attend(mixed, same=None):
    third = mixed.shape[0] // 3
    outs = []
    for at in range(0, third, HEAD_DIM):
        query, key, value = (mixed[at + i * third : at + i * third + HEAD_DIM] for i in range(3))
        weights = jnp.exp(project(key, query) * FACTOR)
        if same is not None:
            weights = jnp.where(same, weights, 0.0)
        weights = (weights / jnp.sum(weights, axis=0, keepdims=True)).astype(jnp.bfloat16)
        outs.append(jnp.dot(value, weights, preferred_element_type=jnp.float32))
    return jnp.concatenate(outs, 0)


def norm_rows(read, full, shift, scale, hidden_ref):
    steps = range(0, full, BLOCK)
    mean = sum(jnp.sum(read(at), axis=0, keepdims=True) for at in steps) / full
    spread = 0.0
    for at in steps:
        center = read(at) - mean
        spread += jnp.sum(center * center, axis=0, keepdims=True)
    inverse = lax.rsqrt(spread / full + EPS)
    for at in steps:
        spot = slice(at, at + BLOCK)
        normal = (read(at) - mean) * inverse
        hidden_ref[spot] = (normal * (1.0 + scale[spot]) + shift[spot]).astype(jnp.bfloat16)


def add_branch(weight, hidden, stream, gate, out_ref, whole_ref):
    for at in range(0, hidden.shape[0], BLOCK):
        spot = slice(at, at + BLOCK)
        branch = jnp.dot(weight(at), hidden, preferred_element_type=jnp.float32)
        total = (stream(at).astype(jnp.float32) + gate[spot] * branch).astype(jnp.bfloat16)
        out_ref[spot] = total
        whole_ref[spot] = total.astype(jnp.float32)


def start_copies(pairs, sems):
    copies = [pltpu.make_async_copy(a, b, sems.at[i]) for i, (a, b) in enumerate(pairs)]
    for copy in copies:
        copy.start()
    return copies


def blocks(weight_ref, held):
    full, cols = held.shape
    spots = [pl.ds(at, BLOCK) for at in range(0, full, BLOCK)]
    return [(weight_ref.at[spot, pl.ds(0, cols)], held.at[spot]) for spot in spots]


def turned_copies_kernel(in_ref, out_ref):
    turned = in_ref[...].T
    for at in range(out_ref.shape[0]):
        out_ref[at] = turned


def side_by_side_kernel(*refs):
    out_ref, at = refs[-1], 0
    for ref in refs[:-1]:
        out_ref[:, at : at + ref.shape[1]] = ref[...]
        at += ref.shape[1]


def opening_kernel(own_ref, late_ref, mod_ref, rows_ref, mod_out_ref):
    rows, cols = own_ref.shape[1], late_ref.shape[1]
    for at in range(rows_ref.shape[0]):
        rows_ref[at, :, :rows] = own_ref[...]
        rows_ref[at, :, rows : rows + cols] = late_ref[...]
    mod_out_ref[...] = mod_ref[...].T


def spatial_kernel(rows_ref, weight_ref, mod_ref, mlp_ref, others_ref, out_ref, late_ref, hidden):
    full, rows = hidden.shape
    depth, units = late_ref.shape[0], mlp_ref.shape[1] // 2
    late_ref[:, :full] = jnp.concatenate(
        [rows_ref[at, :, rows : rows + depth].T for at in range(rows_ref.shape[0])], 1
    )
    for i in range(2):
        for j, ref in enumerate((mlp_ref, others_ref)):
            at = full + (SHARES * i + j) * units
            late_ref[:, at : at + units] = ref[:, i * units : (i + 1) * units]
    read = lambda at: rows_ref[at // BLOCK, :, :rows].astype(jnp.float32)
    norm_rows(read, full, mod_ref[:, 0:1], mod_ref[:, 1:2], hidden)
    mixed = norm_heads(project(weight_ref[...], hidden[...])).astype(jnp.bfloat16)
    block = attend(mixed).astype(out_ref.dtype)
    share = rows // SHARES
    for at in range(out_ref.shape[0]):
        first = at % SHARES * share
        out_ref[at] = block[:, first : first + share]


def spatial_end_kernel(
    spot_ref, gathered_ref, rows_ref, weight_ref, mod_ref, mixed_ref, stream_ref, whole, hidden, held, qkv, sems
):
    full, share = stream_ref.shape
    pairs = blocks(weight_ref, held) + [(weight_ref.at[:, pl.ds(full, qkv.shape[1])], qkv)]
    copies = start_copies(pairs, sems)
    mine = pl.ds(pl.multiple_of(spot_ref[1] * share, share), share)

    def weight(at):
        copies[at // BLOCK].wait()
        return held[at : at + BLOCK]

    add_branch(
        weight,
        gathered_ref[...].reshape(full, share),
        lambda at: rows_ref[at // BLOCK, :, mine],
        mod_ref[:, 2:3],
        stream_ref,
        whole,
    )
    norm_rows(lambda at: whole[at : at + BLOCK], full, mod_ref[:, 3:4], mod_ref[:, 4:5], hidden)
    copies[-1].wait()
    mixed = project(qkv[:, : SHARES * FEATURES], hidden[...])
    mixed = [norm_heads(mixed[at : at + FEATURES]) for at in range(0, SHARES * FEATURES, FEATURES)]
    pack(jnp.concatenate(mixed, 0), mixed_ref, mixed_ref.shape[1])


def temporal_kernel(moved_ref, out_ref):
    mixed = unpack(moved_ref, SHARES * FEATURES).astype(jnp.bfloat16)
    rows = mixed.shape[1]
    spot = lax.broadcasted_iota(jnp.int32, (rows, rows), 0) % PLACE
    spot_q = lax.broadcasted_iota(jnp.int32, (rows, rows), 1) % PLACE
    same = spot == spot_q
    outs = [attend(mixed[at : at + FEATURES], same) for at in range(0, SHARES * FEATURES, FEATURES)]
    pack(jnp.concatenate(outs, 0), out_ref, out_ref.shape[1])


def copies_kernel(spot_ref, moved_ref, out_ref):
    block = unpack(moved_ref, SHARES * BLOCK).astype(out_ref.dtype)
    own = pl.ds(pl.multiple_of(spot_ref[1] * BLOCK, BLOCK), BLOCK)
    other = pl.ds(pl.multiple_of((1 - spot_ref[1]) * BLOCK, BLOCK), BLOCK)
    for at in range(out_ref.shape[0]):
        out_ref[at, own, :] = block[:BLOCK]
        out_ref[at, other, :] = block[BLOCK:]


def mlp_kernel(
    spot_ref, gathered_ref, before_ref, weight_ref, mod_ref, partial_ref, stream, whole, hidden, active,
    held, up, down, sems,
):
    full, rows = stream.shape
    pairs = blocks(weight_ref, held)
    for i, ref in enumerate((up, down)):
        pairs.append((weight_ref.at[:, pl.ds(full + i * up.shape[1], up.shape[1])], ref))
    copies = start_copies(pairs, sems)

    def weight(at):
        copies[at // BLOCK].wait()
        return held[at : at + BLOCK]

    add_branch(
        weight,
        gathered_ref[...].reshape(full, rows),
        lambda at: before_ref[at : at + BLOCK],
        mod_ref[:, 5:6],
        stream,
        whole,
    )
    norm_rows(lambda at: whole[at : at + BLOCK], full, mod_ref[:, 6:7], mod_ref[:, 7:8], hidden)
    copies[-2].wait()
    raised = project(up[...], hidden[...])
    active[...] = jax.nn.gelu(raised, approximate=True).astype(jnp.bfloat16)
    copies[-1].wait()
    for i in range(full // BLOCK):
        spot = slice(i * BLOCK, (i + 1) * BLOCK)
        lowered = jnp.dot(down[spot], active[...], preferred_element_type=jnp.float32)
        carried = jnp.where(spot_ref[0] == i // SHARES, whole[spot], 0.0)
        partial_ref[i] = (carried + mod_ref[spot, 8:9] * lowered).astype(jnp.bfloat16)


def closing_kernel(partial_ref, out_ref):
    count = partial_ref.shape[0]
    for i in range(SHARES):
        share = sum(partial_ref[at].astype(jnp.float32) for at in range(i, count, SHARES))
        out_ref[:, i * share.shape[1] : (i + 1) * share.shape[1]] = share.astype(out_ref.dtype)


HERE = pl.BlockSpec(memory_space=pltpu.VMEM)
THERE = pl.BlockSpec(memory_space=pltpu.HBM)
SCALAR = pl.BlockSpec(memory_space=pltpu.SMEM)


def vmem_call(kernel, out_shape, in_specs, scratch=(), limit=32):
    return pl.pallas_call(
        kernel,
        out_shape=out_shape,
        in_specs=in_specs,
        scratch_shapes=list(scratch),
        compiler_params=pltpu.CompilerParams(vmem_limit_bytes=limit * 2**20),
    )


def per_device(
    latents, modulation, spatial_qkv, spatial_out, temporal_qkv, temporal_out, mlp_up, mlp_down
):
    rows, width = latents.shape[1], latents.shape[2]
    heads_n, frames_n = lax.axis_size("head"), lax.axis_size("frame")
    full = width * heads_n
    depth = spatial_qkv.shape[0]
    units = mlp_up.shape[1]
    lines = heads_n // SHARES
    share = rows // SHARES
    place = lax.axis_index("head").astype(jnp.int32)
    spot = jnp.stack([place // SHARES, place % SHARES])
    array = lambda *shape, dtype=jnp.bfloat16: jax.ShapeDtypeStruct(shape, dtype)
    bf16 = lambda *shape: pltpu.VMEM(shape, jnp.bfloat16)
    f32 = lambda *shape: pltpu.VMEM(shape, jnp.float32)
    sems = lambda count: pltpu.SemaphoreType.DMA((count,))
    spread = lambda copies: lax.all_to_all(copies, "head", 0, 0, tiled=True)
    swap = lambda chunks: lax.all_to_all(chunks, "frame", 0, 0, tiled=True)
    gather_frame = lambda packed: lax.all_gather(packed, "frame", axis=0, tiled=True)
    along_x = [[x * SHARES + y for x in range(lines)] for y in range(SHARES)]
    across_y = [(x * SHARES + y, x * SHARES + 1 - y) for x in range(lines) for y in range(SHARES)]
    wide_qkv = SHARES * 3 * width + -SHARES * 3 * width % LANES

    others_qkv = lax.ppermute(temporal_qkv, "head", across_y)
    out_copies = vmem_call(turned_copies_kernel, array(heads_n, depth, width), [HERE])(spatial_out)
    mlp = vmem_call(side_by_side_kernel, array(depth, 2 * units), [HERE] * 2)(mlp_up, mlp_down.T)
    others = lax.ppermute(mlp, "head", across_y)
    row_copies, mod = vmem_call(
        opening_kernel,
        (
            array(heads_n, width, rows + LANES),
            array(full, modulation.shape[0], dtype=jnp.float32),
        ),
        [HERE] * 3,
    )(latents.reshape(rows, width).T, temporal_out, modulation)

    s_out, row_copies = lax.optimization_barrier((spread(out_copies), row_copies))
    pieces = [
        s_out.transpose(1, 0, 2).reshape(depth, full),
        temporal_qkv.reshape(depth, -1),
        others_qkv.reshape(depth, -1),
        jnp.zeros((depth, -SHARES * 3 * width % LANES), jnp.bfloat16),
    ]
    early = gather_frame(jnp.concatenate(pieces, axis=1))
    stream = spread(row_copies)
    s_qkv = gather_frame(spatial_qkv.reshape(depth, -1))

    attended, late = vmem_call(
        spatial_kernel,
        (array(heads_n, width, share), array(depth, full + 2 * SHARES * units)),
        [HERE] * 5,
        (bf16(full, rows),),
    )(stream, s_qkv, mod, mlp, others)
    late = gather_frame(late)

    mixed, stream = vmem_call(
        spatial_end_kernel,
        (array(frames_n, 112, LANES), array(full, share)),
        [SCALAR, HERE, HERE, THERE, HERE],
        (
            f32(full, share), bf16(full, share), bf16(full, full), bf16(full, wide_qkv),
            sems(full // BLOCK + 1),
        ),
        46,
    )(spot, spread(attended), stream, early, mod)
    attended = vmem_call(temporal_kernel, array(frames_n, 48, LANES), [HERE])(swap(mixed))
    attended = vmem_call(copies_kernel, array(lines, SHARES * width, share), [SCALAR, HERE])(
        spot, swap(attended)
    )
    attended = lax.all_to_all(attended, "head", 0, 0, axis_index_groups=along_x, tiled=True)

    partial = vmem_call(
        mlp_kernel,
        array(heads_n, width, share),
        [SCALAR, HERE, HERE, THERE, HERE],
        (
            bf16(full, share), f32(full, share), bf16(full, share), bf16(SHARES * units, share),
            bf16(full, full), bf16(full, SHARES * units), bf16(full, SHARES * units),
            sems(full // BLOCK + 2),
        ),
        46,
    )(spot, attended, stream, late, mod)
    result = vmem_call(closing_kernel, array(width, rows), [HERE])(spread(partial))
    return result.T.reshape(1, rows, width)


def solution(mesh):
    placed = (
        P(("dp", "frame"), None, "head"),
        P("dp", None),
        P("frame", None, "head"),
        P("head", "frame"),
        P("frame", None, "head"),
        P("head", "frame"),
        P("frame", "head"),
        P("head", "frame"),
    )
    return jax.shard_map(
        per_device,
        mesh=mesh,
        in_specs=placed,
        out_specs=P(("dp", "frame"), None, "head"),
        check_vma=False,
    )
```

```python
import math

import jax
import jax.numpy as jnp
from jax import lax
from jax.experimental import pallas as pl
from jax.experimental.pallas import tpu as pltpu
from jax.sharding import PartitionSpec as P

HEAD_DIM = 72
EPS = 1e-06
FACTOR = 1.0 / math.sqrt(HEAD_DIM)
LANES = 128
SHARES = 2
PLACE = 16
PARTS = LANES // PLACE
BLOCK = 144
STEP = 576
FEATURES = 432


def project(weight, hidden):
    return lax.dot_general(
        weight, hidden, (((0,), (0,)), ((), ())), preferred_element_type=jnp.float32
    )


def exchange(pieces):
    part = lax.broadcasted_iota(jnp.int32, pieces[0].shape, 1) // PLACE
    step = 1
    while step < PARTS:
        held = list(pieces)
        high = (part // step) % 2 == 1
        for i in range(PARTS):
            if i & step:
                continue
            low_piece, high_piece = pieces[i], pieces[i + step]
            held[i] = jnp.where(high, pltpu.roll(high_piece, step * PLACE, 1), low_piece)
            held[i + step] = jnp.where(high, high_piece, pltpu.roll(low_piece, LANES - step * PLACE, 1))
        pieces, step = held, 2 * step
    return pieces


def pack(block, out_ref, group):
    features, rows = block.shape
    if features < PARTS * group:
        block = jnp.concatenate([block, jnp.zeros((PARTS * group - features, rows), block.dtype)], 0)
    for tile in range(rows // LANES):
        cut = block[:, tile * LANES : (tile + 1) * LANES]
        pieces = [cut[at : at + group] for at in range(0, PARTS * group, group)]
        for spot, piece in enumerate(exchange(pieces)):
            out_ref[tile * PARTS + spot] = piece.astype(out_ref.dtype)


def unpack(in_ref, features):
    tiles = []
    for tile in range(in_ref.shape[0] // PARTS):
        held = [in_ref[tile * PARTS + spot].astype(jnp.float32) for spot in range(PARTS)]
        tiles.append(jnp.concatenate(exchange(held), 0)[:features])
    return jnp.concatenate(tiles, 1)


def norm_heads(mixed):
    features, rows = mixed.shape
    parts = mixed.reshape(features // HEAD_DIM, HEAD_DIM, rows)
    scale = lax.rsqrt(jnp.mean(parts * parts, axis=1, keepdims=True) + EPS)
    normed = (parts * scale).reshape(features, rows)
    pairs = 2 * features // 3
    return jnp.concatenate([normed[:pairs], mixed[pairs:]], 0)


def attend(mixed, same=None):
    third = mixed.shape[0] // 3
    outs = []
    for at in range(0, third, HEAD_DIM):
        query, key, value = (mixed[at + i * third : at + i * third + HEAD_DIM] for i in range(3))
        weights = jnp.exp(project(key, query) * FACTOR)
        if same is not None:
            weights = jnp.where(same, weights, 0.0)
        weights = (weights / jnp.sum(weights, axis=0, keepdims=True)).astype(jnp.bfloat16)
        outs.append(jnp.dot(value, weights, preferred_element_type=jnp.float32))
    return jnp.concatenate(outs, 0)


def norm_rows(read, full, shift, scale, hidden_ref):
    steps = range(0, full, BLOCK)
    mean = sum(jnp.sum(read(at), axis=0, keepdims=True) for at in steps) / full
    spread = 0.0
    for at in steps:
        center = read(at) - mean
        spread += jnp.sum(center * center, axis=0, keepdims=True)
    inverse = lax.rsqrt(spread / full + EPS)
    for at in steps:
        spot = slice(at, at + BLOCK)
        normal = (read(at) - mean) * inverse
        hidden_ref[spot] = (normal * (1.0 + scale[spot]) + shift[spot]).astype(jnp.bfloat16)


def add_branch(weight, hidden, stream, gate, out_ref, whole_ref):
    for at in range(0, hidden.shape[0], STEP):
        branch = jnp.dot(weight(at), hidden, preferred_element_type=jnp.float32)
        for inner in range(0, STEP, BLOCK):
            spot = slice(at + inner, at + inner + BLOCK)
            gated = gate[spot] * branch[inner : inner + BLOCK]
            total = (stream(at + inner).astype(jnp.float32) + gated).astype(jnp.bfloat16)
            out_ref[spot] = total
            whole_ref[spot] = total.astype(jnp.float32)


def start_copies(pairs, sems):
    copies = [pltpu.make_async_copy(a, b, sems.at[i]) for i, (a, b) in enumerate(pairs)]
    for copy in copies:
        copy.start()
    return copies


def blocks(weight_ref, held):
    full, cols = held.shape
    spots = [pl.ds(at, STEP) for at in range(0, full, STEP)]
    return [(weight_ref.at[spot, pl.ds(0, cols)], held.at[spot]) for spot in spots]


def turned_copies_kernel(in_ref, out_ref):
    turned = in_ref[...].T
    for at in range(out_ref.shape[0]):
        out_ref[at] = turned


def side_by_side_kernel(*refs):
    out_ref, at = refs[-1], 0
    for ref in refs[:-1]:
        out_ref[:, at : at + ref.shape[1]] = ref[...]
        at += ref.shape[1]


def opening_kernel(own_ref, late_ref, mod_ref, rows_ref, mod_out_ref):
    rows, cols = own_ref.shape[1], late_ref.shape[1]
    for at in range(rows_ref.shape[0]):
        rows_ref[at, :, :rows] = own_ref[...]
        rows_ref[at, :, rows : rows + cols] = late_ref[...]
    mod_out_ref[...] = mod_ref[...].T


def spatial_kernel(rows_ref, weight_ref, mod_ref, mlp_ref, others_ref, out_ref, late_ref, hidden):
    full, rows = hidden.shape
    depth, units = late_ref.shape[0], mlp_ref.shape[1] // 2
    late_ref[:, :full] = jnp.concatenate(
        [rows_ref[at, :, rows : rows + depth].T for at in range(rows_ref.shape[0])], 1
    )
    late_ref[:, full : full + units] = mlp_ref[:, units:]
    late_ref[:, full + units : full + 2 * units] = others_ref[:, units:]
    late_ref[:, full + 2 * units : full + 3 * units] = others_ref[:, :units]
    read = lambda at: rows_ref[at // BLOCK, :, :rows].astype(jnp.float32)
    norm_rows(read, full, mod_ref[:, 0:1], mod_ref[:, 1:2], hidden)
    mixed = norm_heads(project(weight_ref[...], hidden[...])).astype(jnp.bfloat16)
    block = attend(mixed).astype(out_ref.dtype)
    share = rows // SHARES
    for at in range(out_ref.shape[0]):
        first = at % SHARES * share
        out_ref[at] = block[:, first : first + share]


def spatial_end_kernel(
    spot_ref, gathered_ref, rows_ref, weight_ref, mod_ref, mixed_ref, stream_ref, whole, hidden, held, qkv, sems
):
    full, share = stream_ref.shape
    pairs = blocks(weight_ref, held) + [(weight_ref.at[:, pl.ds(full, qkv.shape[1])], qkv)]
    copies = start_copies(pairs, sems)
    mine = pl.ds(pl.multiple_of(spot_ref[1] * share, share), share)

    def weight(at):
        copies[at // STEP].wait()
        return held[at : at + STEP]

    add_branch(
        weight,
        gathered_ref[...].reshape(full, share),
        lambda at: rows_ref[at // BLOCK, :, mine],
        mod_ref[:, 2:3],
        stream_ref,
        whole,
    )
    norm_rows(lambda at: whole[at : at + BLOCK], full, mod_ref[:, 3:4], mod_ref[:, 4:5], hidden)
    copies[-1].wait()
    mixed = project(qkv[:, : SHARES * FEATURES], hidden[...])
    mixed = [norm_heads(mixed[at : at + FEATURES]) for at in range(0, SHARES * FEATURES, FEATURES)]
    pack(jnp.concatenate(mixed, 0), mixed_ref, mixed_ref.shape[1])


def temporal_kernel(moved_ref, out_ref):
    mixed = unpack(moved_ref, SHARES * FEATURES).astype(jnp.bfloat16)
    rows = mixed.shape[1]
    spot = lax.broadcasted_iota(jnp.int32, (rows, rows), 0) % PLACE
    spot_q = lax.broadcasted_iota(jnp.int32, (rows, rows), 1) % PLACE
    same = spot == spot_q
    outs = [attend(mixed[at : at + FEATURES], same) for at in range(0, SHARES * FEATURES, FEATURES)]
    pack(jnp.concatenate(outs, 0), out_ref, out_ref.shape[1])


def copies_kernel(spot_ref, moved_ref, out_ref):
    block = unpack(moved_ref, SHARES * BLOCK).astype(out_ref.dtype)
    own = pl.ds(pl.multiple_of(spot_ref[1] * BLOCK, BLOCK), BLOCK)
    other = pl.ds(pl.multiple_of((1 - spot_ref[1]) * BLOCK, BLOCK), BLOCK)
    for at in range(out_ref.shape[0]):
        out_ref[at, own, :] = block[:BLOCK]
        out_ref[at, other, :] = block[BLOCK:]


def mlp_kernel(
    spot_ref, gathered_ref, before_ref, weight_ref, early_ref, mod_ref, partial_ref, stream, whole, hidden,
    active, held, up, down, sems,
):
    full, rows = stream.shape
    units = active.shape[0] // SHARES
    pairs = blocks(weight_ref, held)
    pairs.append((early_ref.at[:, pl.ds(early_ref.shape[1] - up.shape[2], up.shape[2])], up.at[0]))
    wide = weight_ref.shape[1] - full - SHARES * units
    pairs.append((weight_ref.at[:, pl.ds(full + SHARES * units, wide)], up.at[1, :, pl.ds(0, wide)]))
    for at in range(0, full, STEP):
        rows_at = pl.ds(at, STEP)
        pairs.append((weight_ref.at[rows_at, pl.ds(full, SHARES * units)], down.at[rows_at]))
    copies = start_copies(pairs, sems)
    first = full // STEP

    def weight(at):
        copies[at // STEP].wait()
        return held[at : at + STEP]

    add_branch(
        weight,
        gathered_ref[...].reshape(full, rows),
        lambda at: before_ref[at : at + BLOCK],
        mod_ref[:, 5:6],
        stream,
        whole,
    )
    norm_rows(lambda at: whole[at : at + BLOCK], full, mod_ref[:, 6:7], mod_ref[:, 7:8], hidden)
    for i in range(SHARES):
        copies[first + i].wait()
        raised = project(up[i, :, :units], hidden[...])
        active[i * units : (i + 1) * units] = jax.nn.gelu(raised, approximate=True).astype(jnp.bfloat16)
    for i, at in enumerate(range(0, full, STEP)):
        copies[first + SHARES + i].wait()
        lowered = jnp.dot(down[at : at + STEP], active[...], preferred_element_type=jnp.float32)
        for inner in range(0, STEP, BLOCK):
            spot = slice(at + inner, at + inner + BLOCK)
            place = (at + inner) // BLOCK
            carried = jnp.where(spot_ref[0] == place // SHARES, whole[spot], 0.0)
            gated = mod_ref[spot, 8:9] * lowered[inner : inner + BLOCK]
            partial_ref[place] = (carried + gated).astype(jnp.bfloat16)


def closing_kernel(partial_ref, out_ref):
    count = partial_ref.shape[0]
    for i in range(SHARES):
        share = sum(partial_ref[at].astype(jnp.float32) for at in range(i, count, SHARES))
        out_ref[:, i * share.shape[1] : (i + 1) * share.shape[1]] = share.astype(out_ref.dtype)


HERE = pl.BlockSpec(memory_space=pltpu.VMEM)
THERE = pl.BlockSpec(memory_space=pltpu.HBM)
SCALAR = pl.BlockSpec(memory_space=pltpu.SMEM)


def vmem_call(kernel, out_shape, in_specs, scratch=(), limit=32):
    return pl.pallas_call(
        kernel,
        out_shape=out_shape,
        in_specs=in_specs,
        scratch_shapes=list(scratch),
        compiler_params=pltpu.CompilerParams(vmem_limit_bytes=limit * 2**20),
    )


def per_device(
    latents, modulation, spatial_qkv, spatial_out, temporal_qkv, temporal_out, mlp_up, mlp_down
):
    rows, width = latents.shape[1], latents.shape[2]
    heads_n, frames_n = lax.axis_size("head"), lax.axis_size("frame")
    full = width * heads_n
    depth = spatial_qkv.shape[0]
    units = mlp_up.shape[1]
    lines = heads_n // SHARES
    share = rows // SHARES
    place = lax.axis_index("head").astype(jnp.int32)
    spot = jnp.stack([place // SHARES, place % SHARES])
    array = lambda *shape, dtype=jnp.bfloat16: jax.ShapeDtypeStruct(shape, dtype)
    bf16 = lambda *shape: pltpu.VMEM(shape, jnp.bfloat16)
    f32 = lambda *shape: pltpu.VMEM(shape, jnp.float32)
    sems = lambda count: pltpu.SemaphoreType.DMA((count,))
    spread = lambda copies: lax.all_to_all(copies, "head", 0, 0, tiled=True)
    swap = lambda chunks: lax.all_to_all(chunks, "frame", 0, 0, tiled=True)
    gather_frame = lambda packed: lax.all_gather(packed, "frame", axis=0, tiled=True)
    along_x = [[x * SHARES + y for x in range(lines)] for y in range(SHARES)]
    across_y = [(x * SHARES + y, x * SHARES + 1 - y) for x in range(lines) for y in range(SHARES)]
    pad = lambda a: jnp.pad(a, ((0, 0), (0, -a.shape[1] % LANES)))
    wide_qkv = SHARES * 3 * width + -SHARES * 3 * width % LANES

    others_qkv = lax.ppermute(temporal_qkv, "head", across_y)
    out_copies = vmem_call(turned_copies_kernel, array(heads_n, depth, width), [HERE])(spatial_out)
    mlp = vmem_call(side_by_side_kernel, array(depth, 2 * units), [HERE] * 2)(mlp_up, mlp_down.T)
    others = lax.ppermute(mlp, "head", across_y)
    row_copies, mod = vmem_call(
        opening_kernel,
        (
            array(heads_n, width, rows + LANES),
            array(full, modulation.shape[0], dtype=jnp.float32),
        ),
        [HERE] * 3,
        limit=60,
    )(latents.reshape(rows, width).T, temporal_out, modulation)

    pieces = [
        spread(out_copies).transpose(1, 0, 2).reshape(depth, full),
        temporal_qkv.reshape(depth, -1),
        others_qkv.reshape(depth, -1),
        jnp.zeros((depth, -SHARES * 3 * width % LANES), jnp.bfloat16),
        pad(mlp_up),
    ]
    early = gather_frame(jnp.concatenate(pieces, axis=1))
    stream = spread(row_copies)
    s_qkv = gather_frame(spatial_qkv.reshape(depth, -1))

    attended, late = vmem_call(
        spatial_kernel,
        (array(heads_n, width, share), array(depth, full + 3 * units + -units % LANES)),
        [HERE] * 5,
        (bf16(full, rows),),
    )(stream, s_qkv, mod, mlp, others)
    late = gather_frame(late)

    mixed, stream = vmem_call(
        spatial_end_kernel,
        (array(frames_n, 112, LANES), array(full, share)),
        [SCALAR, HERE, HERE, THERE, HERE],
        (
            f32(full, share), bf16(full, share), bf16(full, full), bf16(full, wide_qkv),
            sems(full // STEP + 1),
        ),
        46,
    )(spot, spread(attended), stream, early, mod)
    attended = vmem_call(temporal_kernel, array(frames_n, 48, LANES), [HERE])(swap(mixed))
    attended = vmem_call(copies_kernel, array(lines, SHARES * width, share), [SCALAR, HERE])(
        spot, swap(attended)
    )
    attended = lax.all_to_all(attended, "head", 0, 0, axis_index_groups=along_x, tiled=True)

    partial = vmem_call(
        mlp_kernel,
        array(heads_n, width, share),
        [SCALAR, HERE, HERE, THERE, THERE, HERE],
        (
            bf16(full, share), f32(full, share), bf16(full, share), bf16(SHARES * units, share),
            bf16(full, full), bf16(SHARES, full, units + -units % LANES), bf16(full, SHARES * units),
            sems(2 * full // STEP + 2),
        ),
        46,
    )(spot, attended, stream, late, early, mod)
    result = vmem_call(closing_kernel, array(width, rows), [HERE])(spread(partial))
    return result.T.reshape(1, rows, width)


def solution(mesh):
    placed = (
        P(("dp", "frame"), None, "head"),
        P("dp", None),
        P("frame", None, "head"),
        P("head", "frame"),
        P("frame", None, "head"),
        P("head", "frame"),
        P("frame", "head"),
        P("head", "frame"),
    )
    return jax.shard_map(
        per_device,
        mesh=mesh,
        in_specs=placed,
        out_specs=P(("dp", "frame"), None, "head"),
        check_vma=False,
    )
```

```python
import math

import jax
import jax.numpy as jnp
from jax import lax
from jax.experimental import pallas as pl
from jax.experimental.pallas import tpu as pltpu
from jax.sharding import PartitionSpec as P

HEAD_DIM = 72
EPS = 1e-06
FACTOR = 1.0 / math.sqrt(HEAD_DIM)
LANES = 128
SHARES = 2
PLACE = 16
PARTS = LANES // PLACE
BLOCK = 144
STEP = 576
UNITS = 512
FEATURES = 432


def project(weight, hidden):
    return lax.dot_general(
        weight, hidden, (((0,), (0,)), ((), ())), preferred_element_type=jnp.float32
    )


def exchange(pieces):
    part = lax.broadcasted_iota(jnp.int32, pieces[0].shape, 1) // PLACE
    step = 1
    while step < PARTS:
        held = list(pieces)
        high = (part // step) % 2 == 1
        for i in range(PARTS):
            if i & step:
                continue
            low_piece, high_piece = pieces[i], pieces[i + step]
            held[i] = jnp.where(high, pltpu.roll(high_piece, step * PLACE, 1), low_piece)
            held[i + step] = jnp.where(high, high_piece, pltpu.roll(low_piece, LANES - step * PLACE, 1))
        pieces, step = held, 2 * step
    return pieces


def pack(block, out_ref, group):
    features, rows = block.shape
    if features < PARTS * group:
        block = jnp.concatenate([block, jnp.zeros((PARTS * group - features, rows), block.dtype)], 0)
    for tile in range(rows // LANES):
        cut = block[:, tile * LANES : (tile + 1) * LANES]
        pieces = [cut[at : at + group] for at in range(0, PARTS * group, group)]
        for spot, piece in enumerate(exchange(pieces)):
            out_ref[tile * PARTS + spot] = piece.astype(out_ref.dtype)


def unpack(in_ref, features):
    tiles = []
    for tile in range(in_ref.shape[0] // PARTS):
        held = [in_ref[tile * PARTS + spot].astype(jnp.float32) for spot in range(PARTS)]
        tiles.append(jnp.concatenate(exchange(held), 0)[:features])
    return jnp.concatenate(tiles, 1)


def norm_heads(mixed):
    features, rows = mixed.shape
    parts = mixed.reshape(features // HEAD_DIM, HEAD_DIM, rows)
    scale = lax.rsqrt(jnp.mean(parts * parts, axis=1, keepdims=True) + EPS)
    normed = (parts * scale).reshape(features, rows)
    pairs = 2 * features // 3
    return jnp.concatenate([normed[:pairs], mixed[pairs:]], 0)


def attend(mixed, same=None):
    third = mixed.shape[0] // 3
    outs = []
    for at in range(0, third, HEAD_DIM):
        query, key, value = (mixed[at + i * third : at + i * third + HEAD_DIM] for i in range(3))
        weights = jnp.exp(project(key, query) * FACTOR)
        if same is not None:
            weights = jnp.where(same, weights, 0.0)
        weights = (weights / jnp.sum(weights, axis=0, keepdims=True)).astype(jnp.bfloat16)
        outs.append(jnp.dot(value, weights, preferred_element_type=jnp.float32))
    return jnp.concatenate(outs, 0)


def norm_rows(read, full, shift, scale, hidden_ref):
    steps = range(0, full, BLOCK)
    mean = sum(jnp.sum(read(at), axis=0, keepdims=True) for at in steps) / full
    spread = 0.0
    for at in steps:
        center = read(at) - mean
        spread += jnp.sum(center * center, axis=0, keepdims=True)
    inverse = lax.rsqrt(spread / full + EPS)
    for at in steps:
        spot = slice(at, at + BLOCK)
        normal = (read(at) - mean) * inverse
        hidden_ref[spot] = (normal * (1.0 + scale[spot]) + shift[spot]).astype(jnp.bfloat16)


def add_branch(weight, hidden, stream, gate, out_ref, whole_ref):
    for at in range(0, hidden.shape[0], STEP):
        branch = jnp.dot(weight(at), hidden, preferred_element_type=jnp.float32)
        for inner in range(0, STEP, BLOCK):
            spot = slice(at + inner, at + inner + BLOCK)
            gated = gate[spot] * branch[inner : inner + BLOCK]
            total = (stream(at + inner).astype(jnp.float32) + gated).astype(jnp.bfloat16)
            out_ref[spot] = total
            whole_ref[spot] = total.astype(jnp.float32)


def start_copies(pairs, sems):
    copies = [pltpu.make_async_copy(a, b, sems.at[i]) for i, (a, b) in enumerate(pairs)]
    for copy in copies:
        copy.start()
    return copies


def blocks(weight_ref, held):
    full, cols = held.shape
    spots = [pl.ds(at, STEP) for at in range(0, full, STEP)]
    return [(weight_ref.at[spot, pl.ds(0, cols)], held.at[spot]) for spot in spots]


def turned_copies_kernel(in_ref, out_ref):
    turned = in_ref[...].T
    for at in range(out_ref.shape[0]):
        out_ref[at] = turned


def side_by_side_kernel(*refs):
    out_ref, at = refs[-1], 0
    for ref in refs[:-1]:
        out_ref[:, at : at + ref.shape[1]] = ref[...]
        at += ref.shape[1]


def opening_kernel(own_ref, late_ref, mod_ref, rows_ref, mod_out_ref):
    rows, cols = own_ref.shape[1], late_ref.shape[1]
    for at in range(rows_ref.shape[0]):
        rows_ref[at, :, :rows] = own_ref[...]
        rows_ref[at, :, rows : rows + cols] = late_ref[...]
    mod_out_ref[...] = mod_ref[...].T


def late_weights_kernel(rows_ref, mlp_ref, others_ref, out_ref):
    depth, units = mlp_ref.shape[0], mlp_ref.shape[1] // 2
    turned = [rows_ref[at, :, :depth].T for at in range(rows_ref.shape[0])]
    pieces = turned + [mlp_ref[:, units:], others_ref[:, units:], mlp_ref[:, UNITS:units], others_ref[:, :units]]
    out_ref[...] = jnp.concatenate(pieces, 1)


def spatial_kernel(rows_ref, weight_ref, mod_ref, out_ref, hidden):
    full, rows = hidden.shape
    read = lambda at: rows_ref[at // BLOCK, :, :rows].astype(jnp.float32)
    norm_rows(read, full, mod_ref[:, 0:1], mod_ref[:, 1:2], hidden)
    mixed = norm_heads(project(weight_ref[...], hidden[...])).astype(jnp.bfloat16)
    block = attend(mixed).astype(out_ref.dtype)
    share = rows // SHARES
    for at in range(out_ref.shape[0]):
        first = at % SHARES * share
        out_ref[at] = block[:, first : first + share]


def spatial_end_kernel(
    spot_ref, gathered_ref, rows_ref, weight_ref, mod_ref, mixed_ref, stream_ref, whole, hidden, held, qkv, sems
):
    full, share = stream_ref.shape
    pairs = blocks(weight_ref, held) + [(weight_ref.at[:, pl.ds(full, qkv.shape[1])], qkv)]
    copies = start_copies(pairs, sems)
    mine = pl.ds(pl.multiple_of(spot_ref[1] * share, share), share)

    def weight(at):
        copies[at // STEP].wait()
        return held[at : at + STEP]

    add_branch(
        weight,
        gathered_ref[...].reshape(full, share),
        lambda at: rows_ref[at // BLOCK, :, mine],
        mod_ref[:, 2:3],
        stream_ref,
        whole,
    )
    norm_rows(lambda at: whole[at : at + BLOCK], full, mod_ref[:, 3:4], mod_ref[:, 4:5], hidden)
    copies[-1].wait()
    mixed = project(qkv[:, : SHARES * FEATURES], hidden[...])
    mixed = [norm_heads(mixed[at : at + FEATURES]) for at in range(0, SHARES * FEATURES, FEATURES)]
    pack(jnp.concatenate(mixed, 0), mixed_ref, mixed_ref.shape[1])


def temporal_kernel(moved_ref, out_ref):
    mixed = unpack(moved_ref, SHARES * FEATURES).astype(jnp.bfloat16)
    rows = mixed.shape[1]
    spot = lax.broadcasted_iota(jnp.int32, (rows, rows), 0) % PLACE
    spot_q = lax.broadcasted_iota(jnp.int32, (rows, rows), 1) % PLACE
    same = spot == spot_q
    outs = [attend(mixed[at : at + FEATURES], same) for at in range(0, SHARES * FEATURES, FEATURES)]
    pack(jnp.concatenate(outs, 0), out_ref, out_ref.shape[1])


def copies_kernel(spot_ref, moved_ref, out_ref):
    block = unpack(moved_ref, SHARES * BLOCK).astype(out_ref.dtype)
    own = pl.ds(pl.multiple_of(spot_ref[1] * BLOCK, BLOCK), BLOCK)
    other = pl.ds(pl.multiple_of((1 - spot_ref[1]) * BLOCK, BLOCK), BLOCK)
    for at in range(out_ref.shape[0]):
        out_ref[at, own, :] = block[:BLOCK]
        out_ref[at, other, :] = block[BLOCK:]


def mlp_kernel(
    spot_ref, gathered_ref, before_ref, weight_ref, early_ref, mod_ref, partial_ref, stream, whole, hidden,
    active, held, up, down, sems,
):
    full, rows = stream.shape
    units = active.shape[0]
    cuts = [(0, UNITS), (UNITS, units - UNITS)]
    pairs = blocks(weight_ref, held)
    pairs.append((early_ref.at[:, pl.ds(early_ref.shape[1] - UNITS, UNITS)], up.at[:, pl.ds(0, UNITS)]))
    rest = units - UNITS
    pairs.append((weight_ref.at[:, pl.ds(full + units, rest)], up.at[:, pl.ds(UNITS, rest)]))
    for at in range(0, full, STEP):
        rows_at = pl.ds(at, STEP)
        pairs.append((weight_ref.at[rows_at, pl.ds(full, units)], down.at[rows_at]))
    copies = start_copies(pairs, sems)
    first = full // STEP

    def weight(at):
        copies[at // STEP].wait()
        return held[at : at + STEP]

    add_branch(
        weight,
        gathered_ref[...].reshape(full, rows),
        lambda at: before_ref[at : at + BLOCK],
        mod_ref[:, 5:6],
        stream,
        whole,
    )
    norm_rows(lambda at: whole[at : at + BLOCK], full, mod_ref[:, 6:7], mod_ref[:, 7:8], hidden)
    for i, (at, count) in enumerate(cuts):
        copies[first + i].wait()
        raised = project(up[:, at : at + count], hidden[...])
        active[at : at + count] = jax.nn.gelu(raised, approximate=True).astype(jnp.bfloat16)
    for i, at in enumerate(range(0, full, STEP)):
        copies[first + len(cuts) + i].wait()
        lowered = jnp.dot(down[at : at + STEP], active[...], preferred_element_type=jnp.float32)
        for inner in range(0, STEP, BLOCK):
            spot = slice(at + inner, at + inner + BLOCK)
            place = (at + inner) // BLOCK
            carried = jnp.where(spot_ref[0] == place // SHARES, whole[spot], 0.0)
            gated = mod_ref[spot, 8:9] * lowered[inner : inner + BLOCK]
            partial_ref[place] = (carried + gated).astype(jnp.bfloat16)


def closing_kernel(partial_ref, out_ref):
    count = partial_ref.shape[0]
    for i in range(SHARES):
        share = sum(partial_ref[at].astype(jnp.float32) for at in range(i, count, SHARES))
        out_ref[:, i * share.shape[1] : (i + 1) * share.shape[1]] = share.astype(out_ref.dtype)


HERE = pl.BlockSpec(memory_space=pltpu.VMEM)
THERE = pl.BlockSpec(memory_space=pltpu.HBM)
SCALAR = pl.BlockSpec(memory_space=pltpu.SMEM)


def vmem_call(kernel, out_shape, in_specs, scratch=(), limit=32):
    return pl.pallas_call(
        kernel,
        out_shape=out_shape,
        in_specs=in_specs,
        scratch_shapes=list(scratch),
        compiler_params=pltpu.CompilerParams(vmem_limit_bytes=limit * 2**20),
    )


def per_device(
    latents, modulation, spatial_qkv, spatial_out, temporal_qkv, temporal_out, mlp_up, mlp_down
):
    rows, width = latents.shape[1], latents.shape[2]
    heads_n, frames_n = lax.axis_size("head"), lax.axis_size("frame")
    full = width * heads_n
    depth = spatial_qkv.shape[0]
    units = mlp_up.shape[1]
    lines = heads_n // SHARES
    share = rows // SHARES
    place = lax.axis_index("head").astype(jnp.int32)
    spot = jnp.stack([place // SHARES, place % SHARES])
    array = lambda *shape, dtype=jnp.bfloat16: jax.ShapeDtypeStruct(shape, dtype)
    bf16 = lambda *shape: pltpu.VMEM(shape, jnp.bfloat16)
    f32 = lambda *shape: pltpu.VMEM(shape, jnp.float32)
    sems = lambda count: pltpu.SemaphoreType.DMA((count,))
    spread = lambda copies: lax.all_to_all(copies, "head", 0, 0, tiled=True)
    swap = lambda chunks: lax.all_to_all(chunks, "frame", 0, 0, tiled=True)
    gather_frame = lambda packed: lax.all_gather(packed, "frame", axis=0, tiled=True)
    along_x = [[x * SHARES + y for x in range(lines)] for y in range(SHARES)]
    across_y = [(x * SHARES + y, x * SHARES + 1 - y) for x in range(lines) for y in range(SHARES)]
    wide_qkv = SHARES * 3 * width + -SHARES * 3 * width % LANES

    others_qkv = lax.ppermute(temporal_qkv, "head", across_y)
    out_copies = vmem_call(turned_copies_kernel, array(heads_n, depth, width), [HERE])(spatial_out)
    mlp = vmem_call(side_by_side_kernel, array(depth, 2 * units), [HERE] * 2)(mlp_up, mlp_down.T)
    others = lax.ppermute(mlp, "head", across_y)
    row_copies, mod = vmem_call(
        opening_kernel,
        (
            array(heads_n, width, rows + LANES),
            array(full, modulation.shape[0], dtype=jnp.float32),
        ),
        [HERE] * 3,
    )(latents.reshape(rows, width).T, temporal_out, modulation)

    pieces = [
        spread(out_copies).transpose(1, 0, 2).reshape(depth, full),
        temporal_qkv.reshape(depth, -1),
        others_qkv.reshape(depth, -1),
        jnp.zeros((depth, -SHARES * 3 * width % LANES), jnp.bfloat16),
        mlp_up[:, :UNITS],
    ]
    early = gather_frame(jnp.concatenate(pieces, axis=1))
    stream = spread(row_copies)
    s_qkv = gather_frame(spatial_qkv.reshape(depth, -1))

    attended = vmem_call(
        spatial_kernel, array(heads_n, width, share), [HERE] * 3, (bf16(full, rows),)
    )(stream, s_qkv, mod)
    t_out, attended = lax.optimization_barrier((stream[:, :, rows:], attended))
    late = vmem_call(
        late_weights_kernel, array(depth, full + 2 * SHARES * units - UNITS), [HERE] * 3
    )(t_out, mlp, others)
    late = gather_frame(late)

    mixed, stream = vmem_call(
        spatial_end_kernel,
        (array(frames_n, 112, LANES), array(full, share)),
        [SCALAR, HERE, HERE, THERE, HERE],
        (
            f32(full, share), bf16(full, share), bf16(full, full), bf16(full, wide_qkv),
            sems(full // STEP + 1),
        ),
        46,
    )(spot, spread(attended), stream, early, mod)
    attended = vmem_call(temporal_kernel, array(frames_n, 48, LANES), [HERE])(swap(mixed))
    attended = vmem_call(copies_kernel, array(lines, SHARES * width, share), [SCALAR, HERE])(
        spot, swap(attended)
    )
    attended = lax.all_to_all(attended, "head", 0, 0, axis_index_groups=along_x, tiled=True)

    partial = vmem_call(
        mlp_kernel,
        array(heads_n, width, share),
        [SCALAR, HERE, HERE, THERE, THERE, HERE],
        (
            bf16(full, share), f32(full, share), bf16(full, share), bf16(SHARES * units, share),
            bf16(full, full), bf16(full, SHARES * units), bf16(full, SHARES * units),
            sems(2 * full // STEP + 2),
        ),
        50,
    )(spot, attended, stream, late, early, mod)
    result = vmem_call(closing_kernel, array(width, rows), [HERE])(spread(partial))
    return result.T.reshape(1, rows, width)


def solution(mesh):
    placed = (
        P(("dp", "frame"), None, "head"),
        P("dp", None),
        P("frame", None, "head"),
        P("head", "frame"),
        P("frame", None, "head"),
        P("head", "frame"),
        P("frame", "head"),
        P("head", "frame"),
    )
    return jax.shard_map(
        per_device,
        mesh=mesh,
        in_specs=placed,
        out_specs=P(("dp", "frame"), None, "head"),
        check_vma=False,
    )
```

```python
import math

import jax
import jax.numpy as jnp
from jax import lax
from jax.experimental import pallas as pl
from jax.experimental.pallas import tpu as pltpu
from jax.sharding import PartitionSpec as P

HEAD_DIM = 72
EPS = 1e-06
FACTOR = 1.0 / math.sqrt(HEAD_DIM)
LANES = 128
SHARES = 2
PLACE = 16
PARTS = LANES // PLACE
BLOCK = 144
STEP = 576
LONG = 1152
UNITS = 512
FEATURES = 432


def project(weight, hidden):
    return lax.dot_general(
        weight, hidden, (((0,), (0,)), ((), ())), preferred_element_type=jnp.float32
    )


def exchange(pieces):
    part = lax.broadcasted_iota(jnp.int32, pieces[0].shape, 1) // PLACE
    step = 1
    while step < PARTS:
        held = list(pieces)
        high = (part // step) % 2 == 1
        for i in range(PARTS):
            if i & step:
                continue
            low_piece, high_piece = pieces[i], pieces[i + step]
            held[i] = jnp.where(high, pltpu.roll(high_piece, step * PLACE, 1), low_piece)
            held[i + step] = jnp.where(high, high_piece, pltpu.roll(low_piece, LANES - step * PLACE, 1))
        pieces, step = held, 2 * step
    return pieces


def pack(block, out_ref, group):
    features, rows = block.shape
    if features < PARTS * group:
        block = jnp.concatenate([block, jnp.zeros((PARTS * group - features, rows), block.dtype)], 0)
    for tile in range(rows // LANES):
        cut = block[:, tile * LANES : (tile + 1) * LANES]
        pieces = [cut[at : at + group] for at in range(0, PARTS * group, group)]
        for spot, piece in enumerate(exchange(pieces)):
            out_ref[tile * PARTS + spot] = piece.astype(out_ref.dtype)


def unpack(in_ref, features):
    tiles = []
    for tile in range(in_ref.shape[0] // PARTS):
        held = [in_ref[tile * PARTS + spot].astype(jnp.float32) for spot in range(PARTS)]
        tiles.append(jnp.concatenate(exchange(held), 0)[:features])
    return jnp.concatenate(tiles, 1)


def norm_heads(mixed):
    features, rows = mixed.shape
    parts = mixed.reshape(features // HEAD_DIM, HEAD_DIM, rows)
    scale = lax.rsqrt(jnp.mean(parts * parts, axis=1, keepdims=True) + EPS)
    normed = (parts * scale).reshape(features, rows)
    pairs = 2 * features // 3
    return jnp.concatenate([normed[:pairs], mixed[pairs:]], 0)


def attend(mixed, same=None):
    third = mixed.shape[0] // 3
    outs = []
    for at in range(0, third, HEAD_DIM):
        query, key, value = (mixed[at + i * third : at + i * third + HEAD_DIM] for i in range(3))
        weights = jnp.exp(project(key, query) * FACTOR)
        if same is not None:
            weights = jnp.where(same, weights, 0.0)
        weights = (weights / jnp.sum(weights, axis=0, keepdims=True)).astype(jnp.bfloat16)
        outs.append(jnp.dot(value, weights, preferred_element_type=jnp.float32))
    return jnp.concatenate(outs, 0)


def norm_rows(read, full, shift, scale, hidden_ref):
    steps = range(0, full, BLOCK)
    mean = sum(jnp.sum(read(at), axis=0, keepdims=True) for at in steps) / full
    spread = 0.0
    for at in steps:
        center = read(at) - mean
        spread += jnp.sum(center * center, axis=0, keepdims=True)
    inverse = lax.rsqrt(spread / full + EPS)
    for at in steps:
        spot = slice(at, at + BLOCK)
        normal = (read(at) - mean) * inverse
        hidden_ref[spot] = (normal * (1.0 + scale[spot]) + shift[spot]).astype(jnp.bfloat16)


def add_branch(weight, hidden, stream, gate, out_ref, whole_ref, step=STEP):
    for at in range(0, hidden.shape[0], step):
        branch = jnp.dot(weight(at), hidden, preferred_element_type=jnp.float32)
        for inner in range(0, step, BLOCK):
            spot = slice(at + inner, at + inner + BLOCK)
            gated = gate[spot] * branch[inner : inner + BLOCK]
            total = (stream(at + inner).astype(jnp.float32) + gated).astype(jnp.bfloat16)
            out_ref[spot] = total
            whole_ref[spot] = total.astype(jnp.float32)


def start_copies(pairs, sems):
    copies = [pltpu.make_async_copy(a, b, sems.at[i]) for i, (a, b) in enumerate(pairs)]
    for copy in copies:
        copy.start()
    return copies


def blocks(weight_ref, held, step=STEP):
    full, cols = held.shape
    spots = [pl.ds(at, step) for at in range(0, full, step)]
    return [(weight_ref.at[spot, pl.ds(0, cols)], held.at[spot]) for spot in spots]


def turned_copies_kernel(in_ref, out_ref):
    turned = in_ref[...].T
    for at in range(out_ref.shape[0]):
        out_ref[at] = turned


def side_by_side_kernel(*refs):
    out_ref, at = refs[-1], 0
    for ref in refs[:-1]:
        out_ref[:, at : at + ref.shape[1]] = ref[...]
        at += ref.shape[1]


def opening_kernel(own_ref, late_ref, mod_ref, rows_ref, mod_out_ref):
    rows, cols = own_ref.shape[1], late_ref.shape[1]
    for at in range(rows_ref.shape[0]):
        rows_ref[at, :, :rows] = own_ref[...]
        rows_ref[at, :, rows : rows + cols] = late_ref[...]
    mod_out_ref[...] = mod_ref[...].T


def late_weights_kernel(rows_ref, mlp_ref, others_ref, out_ref):
    depth, units = mlp_ref.shape[0], mlp_ref.shape[1] // 2
    turned = [rows_ref[at, :, :depth].T for at in range(rows_ref.shape[0])]
    pieces = turned + [mlp_ref[:, units:], others_ref[:, units:], mlp_ref[:, UNITS:units], others_ref[:, :units]]
    out_ref[...] = jnp.concatenate(pieces, 1)


def spatial_kernel(rows_ref, weight_ref, mod_ref, out_ref, hidden):
    full, rows = hidden.shape
    read = lambda at: rows_ref[at // BLOCK, :, :rows].astype(jnp.float32)
    norm_rows(read, full, mod_ref[:, 0:1], mod_ref[:, 1:2], hidden)
    mixed = norm_heads(project(weight_ref[...], hidden[...])).astype(jnp.bfloat16)
    block = attend(mixed).astype(out_ref.dtype)
    share = rows // SHARES
    for at in range(out_ref.shape[0]):
        first = at % SHARES * share
        out_ref[at] = block[:, first : first + share]


def spatial_end_kernel(
    spot_ref, gathered_ref, rows_ref, weight_ref, mod_ref, mixed_ref, stream_ref, whole, hidden, held, qkv, sems
):
    full, share = stream_ref.shape
    pairs = blocks(weight_ref, held) + [(weight_ref.at[:, pl.ds(full, qkv.shape[1])], qkv)]
    copies = start_copies(pairs, sems)
    mine = pl.ds(pl.multiple_of(spot_ref[1] * share, share), share)

    def weight(at):
        copies[at // STEP].wait()
        return held[at : at + STEP]

    add_branch(
        weight,
        gathered_ref[...].reshape(full, share),
        lambda at: rows_ref[at // BLOCK, :, mine],
        mod_ref[:, 2:3],
        stream_ref,
        whole,
    )
    norm_rows(lambda at: whole[at : at + BLOCK], full, mod_ref[:, 3:4], mod_ref[:, 4:5], hidden)
    copies[-1].wait()
    mixed = project(qkv[:, : SHARES * FEATURES], hidden[...])
    mixed = [norm_heads(mixed[at : at + FEATURES]) for at in range(0, SHARES * FEATURES, FEATURES)]
    pack(jnp.concatenate(mixed, 0), mixed_ref, mixed_ref.shape[1])


def temporal_kernel(moved_ref, out_ref):
    mixed = unpack(moved_ref, SHARES * FEATURES).astype(jnp.bfloat16)
    rows = mixed.shape[1]
    spot = lax.broadcasted_iota(jnp.int32, (rows, rows), 0) % PLACE
    spot_q = lax.broadcasted_iota(jnp.int32, (rows, rows), 1) % PLACE
    same = spot == spot_q
    outs = [attend(mixed[at : at + FEATURES], same) for at in range(0, SHARES * FEATURES, FEATURES)]
    pack(jnp.concatenate(outs, 0), out_ref, out_ref.shape[1])


def copies_kernel(spot_ref, moved_ref, out_ref):
    block = unpack(moved_ref, SHARES * BLOCK).astype(out_ref.dtype)
    own = pl.ds(pl.multiple_of(spot_ref[1] * BLOCK, BLOCK), BLOCK)
    other = pl.ds(pl.multiple_of((1 - spot_ref[1]) * BLOCK, BLOCK), BLOCK)
    for at in range(out_ref.shape[0]):
        out_ref[at, own, :] = block[:BLOCK]
        out_ref[at, other, :] = block[BLOCK:]


def mlp_kernel(
    spot_ref, gathered_ref, before_ref, weight_ref, early_ref, mod_ref, partial_ref, stream, whole, hidden,
    active, held, up, down, sems,
):
    full, rows = stream.shape
    units = active.shape[0]
    cuts = [(0, UNITS), (UNITS, units - UNITS)]
    pairs = blocks(weight_ref, held, LONG)
    pairs.append((early_ref.at[:, pl.ds(early_ref.shape[1] - UNITS, UNITS)], up.at[:, pl.ds(0, UNITS)]))
    rest = units - UNITS
    pairs.append((weight_ref.at[:, pl.ds(full + units, rest)], up.at[:, pl.ds(UNITS, rest)]))
    for at in range(0, full, LONG):
        rows_at = pl.ds(at, LONG)
        pairs.append((weight_ref.at[rows_at, pl.ds(full, units)], down.at[rows_at]))
    copies = start_copies(pairs, sems)
    first = full // LONG

    def weight(at):
        copies[at // LONG].wait()
        return held[at : at + LONG]

    add_branch(
        weight,
        gathered_ref[...].reshape(full, rows),
        lambda at: before_ref[at : at + BLOCK],
        mod_ref[:, 5:6],
        stream,
        whole,
        LONG,
    )
    norm_rows(lambda at: whole[at : at + BLOCK], full, mod_ref[:, 6:7], mod_ref[:, 7:8], hidden)
    for i, (at, count) in enumerate(cuts):
        copies[first + i].wait()
        raised = project(up[:, at : at + count], hidden[...])
        active[at : at + count] = jax.nn.gelu(raised, approximate=True).astype(jnp.bfloat16)
    for i, at in enumerate(range(0, full, LONG)):
        copies[first + len(cuts) + i].wait()
        lowered = jnp.dot(down[at : at + LONG], active[...], preferred_element_type=jnp.float32)
        for inner in range(0, LONG, BLOCK):
            spot = slice(at + inner, at + inner + BLOCK)
            place = (at + inner) // BLOCK
            carried = jnp.where(spot_ref[0] == place // SHARES, whole[spot], 0.0)
            gated = mod_ref[spot, 8:9] * lowered[inner : inner + BLOCK]
            partial_ref[place] = (carried + gated).astype(jnp.bfloat16)


def closing_kernel(partial_ref, out_ref):
    count = partial_ref.shape[0]
    for i in range(SHARES):
        share = sum(partial_ref[at].astype(jnp.float32) for at in range(i, count, SHARES))
        out_ref[:, i * share.shape[1] : (i + 1) * share.shape[1]] = share.astype(out_ref.dtype)


HERE = pl.BlockSpec(memory_space=pltpu.VMEM)
THERE = pl.BlockSpec(memory_space=pltpu.HBM)
SCALAR = pl.BlockSpec(memory_space=pltpu.SMEM)


def vmem_call(kernel, out_shape, in_specs, scratch=(), limit=32):
    return pl.pallas_call(
        kernel,
        out_shape=out_shape,
        in_specs=in_specs,
        scratch_shapes=list(scratch),
        compiler_params=pltpu.CompilerParams(vmem_limit_bytes=limit * 2**20),
    )


def per_device(
    latents, modulation, spatial_qkv, spatial_out, temporal_qkv, temporal_out, mlp_up, mlp_down
):
    rows, width = latents.shape[1], latents.shape[2]
    heads_n, frames_n = lax.axis_size("head"), lax.axis_size("frame")
    full = width * heads_n
    depth = spatial_qkv.shape[0]
    units = mlp_up.shape[1]
    lines = heads_n // SHARES
    share = rows // SHARES
    place = lax.axis_index("head").astype(jnp.int32)
    spot = jnp.stack([place // SHARES, place % SHARES])
    array = lambda *shape, dtype=jnp.bfloat16: jax.ShapeDtypeStruct(shape, dtype)
    bf16 = lambda *shape: pltpu.VMEM(shape, jnp.bfloat16)
    f32 = lambda *shape: pltpu.VMEM(shape, jnp.float32)
    sems = lambda count: pltpu.SemaphoreType.DMA((count,))
    spread = lambda copies: lax.all_to_all(copies, "head", 0, 0, tiled=True)
    swap = lambda chunks: lax.all_to_all(chunks, "frame", 0, 0, tiled=True)
    gather_frame = lambda packed: lax.all_gather(packed, "frame", axis=0, tiled=True)
    along_x = [[x * SHARES + y for x in range(lines)] for y in range(SHARES)]
    across_y = [(x * SHARES + y, x * SHARES + 1 - y) for x in range(lines) for y in range(SHARES)]
    wide_qkv = SHARES * 3 * width + -SHARES * 3 * width % LANES

    others_qkv = lax.ppermute(temporal_qkv, "head", across_y)
    out_copies = vmem_call(turned_copies_kernel, array(heads_n, depth, width), [HERE])(spatial_out)
    mlp = vmem_call(side_by_side_kernel, array(depth, 2 * units), [HERE] * 2)(mlp_up, mlp_down.T)
    others = lax.ppermute(mlp, "head", across_y)
    row_copies, mod = vmem_call(
        opening_kernel,
        (
            array(heads_n, width, rows + LANES),
            array(full, modulation.shape[0], dtype=jnp.float32),
        ),
        [HERE] * 3,
    )(latents.reshape(rows, width).T, temporal_out, modulation)

    pieces = [
        spread(out_copies).transpose(1, 0, 2).reshape(depth, full),
        temporal_qkv.reshape(depth, -1),
        others_qkv.reshape(depth, -1),
        jnp.zeros((depth, -SHARES * 3 * width % LANES), jnp.bfloat16),
        mlp_up[:, :UNITS],
    ]
    early = gather_frame(jnp.concatenate(pieces, axis=1))
    stream = spread(row_copies)
    s_qkv = gather_frame(spatial_qkv.reshape(depth, -1))

    attended = vmem_call(
        spatial_kernel, array(heads_n, width, share), [HERE] * 3, (bf16(full, rows),)
    )(stream, s_qkv, mod)
    t_out, attended = lax.optimization_barrier((stream[:, :, rows:], attended))
    late = vmem_call(
        late_weights_kernel, array(depth, full + 2 * SHARES * units - UNITS), [HERE] * 3
    )(t_out, mlp, others)
    late = gather_frame(late)

    mixed, stream = vmem_call(
        spatial_end_kernel,
        (array(frames_n, 112, LANES), array(full, share)),
        [SCALAR, HERE, HERE, THERE, HERE],
        (
            f32(full, share), bf16(full, share), bf16(full, full), bf16(full, wide_qkv),
            sems(full // STEP + 1),
        ),
        46,
    )(spot, spread(attended), stream, early, mod)
    attended = vmem_call(temporal_kernel, array(frames_n, 48, LANES), [HERE])(swap(mixed))
    attended = vmem_call(copies_kernel, array(lines, SHARES * width, share), [SCALAR, HERE])(
        spot, swap(attended)
    )
    attended = lax.all_to_all(attended, "head", 0, 0, axis_index_groups=along_x, tiled=True)

    partial = vmem_call(
        mlp_kernel,
        array(heads_n, width, share),
        [SCALAR, HERE, HERE, THERE, THERE, HERE],
        (
            bf16(full, share), f32(full, share), bf16(full, share), bf16(SHARES * units, share),
            bf16(full, full), bf16(full, SHARES * units), bf16(full, SHARES * units),
            sems(2 * full // LONG + 2),
        ),
        50,
    )(spot, attended, stream, late, early, mod)
    result = vmem_call(closing_kernel, array(width, rows), [HERE])(spread(partial))
    return result.T.reshape(1, rows, width)


def solution(mesh):
    placed = (
        P(("dp", "frame"), None, "head"),
        P("dp", None),
        P("frame", None, "head"),
        P("head", "frame"),
        P("frame", None, "head"),
        P("head", "frame"),
        P("frame", "head"),
        P("head", "frame"),
    )
    return jax.shard_map(
        per_device,
        mesh=mesh,
        in_specs=placed,
        out_specs=P(("dp", "frame"), None, "head"),
        check_vma=False,
    )
```

```python
import math

import jax
import jax.numpy as jnp
from jax import lax
from jax.experimental import pallas as pl
from jax.experimental.pallas import tpu as pltpu
from jax.sharding import PartitionSpec as P

HEAD_DIM = 72
EPS = 1e-06
FACTOR = 1.0 / math.sqrt(HEAD_DIM)
LANES = 128
SHARES = 2
PLACE = 16
PARTS = LANES // PLACE
BLOCK = 144
STEP = 576
LONG = 1152
UNITS = 512
FEATURES = 432


def project(weight, hidden):
    return lax.dot_general(
        weight, hidden, (((0,), (0,)), ((), ())), preferred_element_type=jnp.float32
    )


def exchange(pieces):
    part = lax.broadcasted_iota(jnp.int32, pieces[0].shape, 1) // PLACE
    step = 1
    while step < PARTS:
        held = list(pieces)
        high = (part // step) % 2 == 1
        for i in range(PARTS):
            if i & step:
                continue
            low_piece, high_piece = pieces[i], pieces[i + step]
            held[i] = jnp.where(high, pltpu.roll(high_piece, step * PLACE, 1), low_piece)
            held[i + step] = jnp.where(high, high_piece, pltpu.roll(low_piece, LANES - step * PLACE, 1))
        pieces, step = held, 2 * step
    return pieces


def pack(block, out_ref, group):
    features, rows = block.shape
    if features < PARTS * group:
        block = jnp.concatenate([block, jnp.zeros((PARTS * group - features, rows), block.dtype)], 0)
    for tile in range(rows // LANES):
        cut = block[:, tile * LANES : (tile + 1) * LANES]
        pieces = [cut[at : at + group] for at in range(0, PARTS * group, group)]
        for spot, piece in enumerate(exchange(pieces)):
            out_ref[tile * PARTS + spot] = piece.astype(out_ref.dtype)


def unpack(in_ref, features):
    tiles = []
    for tile in range(in_ref.shape[0] // PARTS):
        held = [in_ref[tile * PARTS + spot].astype(jnp.float32) for spot in range(PARTS)]
        tiles.append(jnp.concatenate(exchange(held), 0)[:features])
    return jnp.concatenate(tiles, 1)


def norm_heads(mixed):
    features, rows = mixed.shape
    parts = mixed.reshape(features // HEAD_DIM, HEAD_DIM, rows)
    scale = lax.rsqrt(jnp.mean(parts * parts, axis=1, keepdims=True) + EPS)
    normed = (parts * scale).reshape(features, rows)
    pairs = 2 * features // 3
    return jnp.concatenate([normed[:pairs], mixed[pairs:]], 0)


def attend(mixed, same=None):
    third = mixed.shape[0] // 3
    outs = []
    for at in range(0, third, HEAD_DIM):
        query, key, value = (mixed[at + i * third : at + i * third + HEAD_DIM] for i in range(3))
        weights = jnp.exp(project(key, query) * FACTOR)
        if same is not None:
            weights = jnp.where(same, weights, 0.0)
        weights = (weights / jnp.sum(weights, axis=0, keepdims=True)).astype(jnp.bfloat16)
        outs.append(jnp.dot(value, weights, preferred_element_type=jnp.float32))
    return jnp.concatenate(outs, 0)


def norm_rows(read, full, shift, scale, hidden_ref):
    steps = range(0, full, BLOCK)
    mean = sum(jnp.sum(read(at), axis=0, keepdims=True) for at in steps) / full
    spread = 0.0
    for at in steps:
        center = read(at) - mean
        spread += jnp.sum(center * center, axis=0, keepdims=True)
    inverse = lax.rsqrt(spread / full + EPS)
    for at in steps:
        spot = slice(at, at + BLOCK)
        normal = (read(at) - mean) * inverse
        hidden_ref[spot] = (normal * (1.0 + scale[spot]) + shift[spot]).astype(jnp.bfloat16)


def add_branch(weight, hidden, stream, gate, out_ref, whole_ref, step=STEP):
    for at in range(0, hidden.shape[0], step):
        branch = jnp.dot(weight(at), hidden, preferred_element_type=jnp.float32)
        for inner in range(0, step, BLOCK):
            spot = slice(at + inner, at + inner + BLOCK)
            gated = gate[spot] * branch[inner : inner + BLOCK]
            total = (stream(at + inner).astype(jnp.float32) + gated).astype(jnp.bfloat16)
            out_ref[spot] = total
            whole_ref[spot] = total.astype(jnp.float32)


def start_copies(pairs, sems):
    copies = [pltpu.make_async_copy(a, b, sems.at[i]) for i, (a, b) in enumerate(pairs)]
    for copy in copies:
        copy.start()
    return copies


def blocks(weight_ref, held, step=STEP):
    full, cols = held.shape
    spots = [pl.ds(at, step) for at in range(0, full, step)]
    return [(weight_ref.at[spot, pl.ds(0, cols)], held.at[spot]) for spot in spots]


def turned_copies_kernel(in_ref, out_ref):
    turned = in_ref[...].T
    for at in range(out_ref.shape[0]):
        out_ref[at] = turned


def side_by_side_kernel(*refs):
    out_ref, at = refs[-1], 0
    for ref in refs[:-1]:
        out_ref[:, at : at + ref.shape[1]] = ref[...]
        at += ref.shape[1]


def opening_kernel(own_ref, late_ref, mod_ref, rows_ref, mod_out_ref):
    rows, cols = own_ref.shape[1], late_ref.shape[1]
    for at in range(rows_ref.shape[0]):
        rows_ref[at, :, :rows] = own_ref[...]
        rows_ref[at, :, rows : rows + cols] = late_ref[...]
    mod_out_ref[...] = mod_ref[...].T


def spatial_kernel(rows_ref, weight_ref, mod_ref, out_ref, late_ref, hidden):
    full, rows = hidden.shape
    depth = late_ref.shape[0]
    late_ref[...] = jnp.concatenate(
        [rows_ref[at, :, rows : rows + depth].T for at in range(rows_ref.shape[0])], 1
    )
    read = lambda at: rows_ref[at // BLOCK, :, :rows].astype(jnp.float32)
    norm_rows(read, full, mod_ref[:, 0:1], mod_ref[:, 1:2], hidden)
    mixed = norm_heads(project(weight_ref[...], hidden[...])).astype(jnp.bfloat16)
    block = attend(mixed).astype(out_ref.dtype)
    share = rows // SHARES
    for at in range(out_ref.shape[0]):
        first = at % SHARES * share
        out_ref[at] = block[:, first : first + share]


def spatial_end_kernel(
    spot_ref, gathered_ref, rows_ref, weight_ref, mod_ref, mixed_ref, stream_ref, whole, hidden, held, qkv, sems
):
    full, share = stream_ref.shape
    pairs = blocks(weight_ref, held) + [(weight_ref.at[:, pl.ds(full, qkv.shape[1])], qkv)]
    copies = start_copies(pairs, sems)
    mine = pl.ds(pl.multiple_of(spot_ref[1] * share, share), share)

    def weight(at):
        copies[at // STEP].wait()
        return held[at : at + STEP]

    add_branch(
        weight,
        gathered_ref[...].reshape(full, share),
        lambda at: rows_ref[at // BLOCK, :, mine],
        mod_ref[:, 2:3],
        stream_ref,
        whole,
    )
    norm_rows(lambda at: whole[at : at + BLOCK], full, mod_ref[:, 3:4], mod_ref[:, 4:5], hidden)
    copies[-1].wait()
    mixed = project(qkv[:, : SHARES * FEATURES], hidden[...])
    mixed = [norm_heads(mixed[at : at + FEATURES]) for at in range(0, SHARES * FEATURES, FEATURES)]
    pack(jnp.concatenate(mixed, 0), mixed_ref, mixed_ref.shape[1])


def temporal_kernel(moved_ref, out_ref):
    mixed = unpack(moved_ref, SHARES * FEATURES).astype(jnp.bfloat16)
    rows = mixed.shape[1]
    spot = lax.broadcasted_iota(jnp.int32, (rows, rows), 0) % PLACE
    spot_q = lax.broadcasted_iota(jnp.int32, (rows, rows), 1) % PLACE
    same = spot == spot_q
    outs = [attend(mixed[at : at + FEATURES], same) for at in range(0, SHARES * FEATURES, FEATURES)]
    pack(jnp.concatenate(outs, 0), out_ref, out_ref.shape[1])


def copies_kernel(spot_ref, moved_ref, out_ref):
    block = unpack(moved_ref, SHARES * BLOCK).astype(out_ref.dtype)
    own = pl.ds(pl.multiple_of(spot_ref[1] * BLOCK, BLOCK), BLOCK)
    other = pl.ds(pl.multiple_of((1 - spot_ref[1]) * BLOCK, BLOCK), BLOCK)
    for at in range(out_ref.shape[0]):
        out_ref[at, own, :] = block[:BLOCK]
        out_ref[at, other, :] = block[BLOCK:]


def mlp_kernel(
    spot_ref, gathered_ref, before_ref, weight_ref, early_ref, mod_ref, partial_ref, stream, whole, hidden,
    active, held, up, down, sems,
):
    full, rows = stream.shape
    units = active.shape[0]
    cuts = [(0, UNITS), (UNITS, units - UNITS)]
    pairs = blocks(weight_ref, held, LONG)
    pairs.append((early_ref.at[:, pl.ds(early_ref.shape[1] - UNITS, UNITS)], up.at[:, pl.ds(0, UNITS)]))
    rest = units - UNITS
    pairs.append((weight_ref.at[:, pl.ds(full + units, rest)], up.at[:, pl.ds(UNITS, rest)]))
    for at in range(0, full, LONG):
        rows_at = pl.ds(at, LONG)
        pairs.append((weight_ref.at[rows_at, pl.ds(full, units)], down.at[rows_at]))
    copies = start_copies(pairs, sems)
    first = full // LONG

    def weight(at):
        copies[at // LONG].wait()
        return held[at : at + LONG]

    add_branch(
        weight,
        gathered_ref[...].reshape(full, rows),
        lambda at: before_ref[at : at + BLOCK],
        mod_ref[:, 5:6],
        stream,
        whole,
        LONG,
    )
    norm_rows(lambda at: whole[at : at + BLOCK], full, mod_ref[:, 6:7], mod_ref[:, 7:8], hidden)
    for i, (at, count) in enumerate(cuts):
        copies[first + i].wait()
        raised = project(up[:, at : at + count], hidden[...])
        raised = jax.nn.gelu(raised, approximate=True).astype(jnp.bfloat16)
        if at == 0:
            active[:count] = raised
        else:
            active[units // SHARES :] = raised[: units // SHARES]
            active[UNITS : units // SHARES] = raised[units // SHARES :]
    for i, at in enumerate(range(0, full, LONG)):
        copies[first + len(cuts) + i].wait()
        lowered = jnp.dot(down[at : at + LONG], active[...], preferred_element_type=jnp.float32)
        for inner in range(0, LONG, BLOCK):
            spot = slice(at + inner, at + inner + BLOCK)
            place = (at + inner) // BLOCK
            carried = jnp.where(spot_ref[0] == place // SHARES, whole[spot], 0.0)
            gated = mod_ref[spot, 8:9] * lowered[inner : inner + BLOCK]
            partial_ref[place] = (carried + gated).astype(jnp.bfloat16)


def closing_kernel(partial_ref, out_ref):
    count = partial_ref.shape[0]
    for i in range(SHARES):
        share = sum(partial_ref[at].astype(jnp.float32) for at in range(i, count, SHARES))
        out_ref[:, i * share.shape[1] : (i + 1) * share.shape[1]] = share.astype(out_ref.dtype)


HERE = pl.BlockSpec(memory_space=pltpu.VMEM)
THERE = pl.BlockSpec(memory_space=pltpu.HBM)
SCALAR = pl.BlockSpec(memory_space=pltpu.SMEM)


def vmem_call(kernel, out_shape, in_specs, scratch=(), limit=32):
    return pl.pallas_call(
        kernel,
        out_shape=out_shape,
        in_specs=in_specs,
        scratch_shapes=list(scratch),
        compiler_params=pltpu.CompilerParams(vmem_limit_bytes=limit * 2**20),
    )


def per_device(
    latents, modulation, spatial_qkv, spatial_out, temporal_qkv, temporal_out, mlp_up, mlp_down
):
    rows, width = latents.shape[1], latents.shape[2]
    heads_n, frames_n = lax.axis_size("head"), lax.axis_size("frame")
    full = width * heads_n
    depth = spatial_qkv.shape[0]
    units = mlp_up.shape[1]
    lines = heads_n // SHARES
    share = rows // SHARES
    place = lax.axis_index("head").astype(jnp.int32)
    spot = jnp.stack([place // SHARES, place % SHARES])
    array = lambda *shape, dtype=jnp.bfloat16: jax.ShapeDtypeStruct(shape, dtype)
    bf16 = lambda *shape: pltpu.VMEM(shape, jnp.bfloat16)
    f32 = lambda *shape: pltpu.VMEM(shape, jnp.float32)
    sems = lambda count: pltpu.SemaphoreType.DMA((count,))
    spread = lambda copies: lax.all_to_all(copies, "head", 0, 0, tiled=True)
    swap = lambda chunks: lax.all_to_all(chunks, "frame", 0, 0, tiled=True)
    gather_frame = lambda packed: lax.all_gather(packed, "frame", axis=0, tiled=True)
    along_x = [[x * SHARES + y for x in range(lines)] for y in range(SHARES)]
    across_y = [(x * SHARES + y, x * SHARES + 1 - y) for x in range(lines) for y in range(SHARES)]
    wide_qkv = SHARES * 3 * width + -SHARES * 3 * width % LANES

    others_qkv = lax.ppermute(temporal_qkv, "head", across_y)
    out_copies = vmem_call(turned_copies_kernel, array(heads_n, depth, width), [HERE])(spatial_out)
    mlp = vmem_call(side_by_side_kernel, array(depth, 2 * units), [HERE] * 2)(mlp_down.T, mlp_up)
    row_copies, mod = vmem_call(
        opening_kernel,
        (
            array(heads_n, width, rows + LANES),
            array(full, modulation.shape[0], dtype=jnp.float32),
        ),
        [HERE] * 3,
    )(latents.reshape(rows, width).T, temporal_out, modulation)

    pieces = [
        spread(out_copies).transpose(1, 0, 2).reshape(depth, full),
        temporal_qkv.reshape(depth, -1),
        others_qkv.reshape(depth, -1),
        jnp.zeros((depth, -SHARES * 3 * width % LANES), jnp.bfloat16),
        mlp_up[:, :UNITS],
    ]
    early = gather_frame(jnp.concatenate(pieces, axis=1))
    stream = spread(row_copies)
    s_qkv = gather_frame(spatial_qkv.reshape(depth, -1))

    s_qkv, mlp = lax.optimization_barrier((s_qkv, mlp))
    others = lax.ppermute(mlp, "head", across_y)

    attended, t_out = vmem_call(
        spatial_kernel,
        (array(heads_n, width, share), array(depth, full)),
        [HERE] * 3,
        (bf16(full, rows),),
    )(stream, s_qkv, mod)
    late = [t_out, mlp[:, :units], others, mlp[:, units + UNITS :]]
    late = gather_frame(jnp.concatenate(late, axis=1))

    mixed, stream = vmem_call(
        spatial_end_kernel,
        (array(frames_n, 112, LANES), array(full, share)),
        [SCALAR, HERE, HERE, THERE, HERE],
        (
            f32(full, share), bf16(full, share), bf16(full, full), bf16(full, wide_qkv),
            sems(full // STEP + 1),
        ),
        46,
    )(spot, spread(attended), stream, early, mod)
    attended = vmem_call(temporal_kernel, array(frames_n, 48, LANES), [HERE])(swap(mixed))
    attended = vmem_call(copies_kernel, array(lines, SHARES * width, share), [SCALAR, HERE])(
        spot, swap(attended)
    )
    attended = lax.all_to_all(attended, "head", 0, 0, axis_index_groups=along_x, tiled=True)

    partial = vmem_call(
        mlp_kernel,
        array(heads_n, width, share),
        [SCALAR, HERE, HERE, THERE, THERE, HERE],
        (
            bf16(full, share), f32(full, share), bf16(full, share), bf16(SHARES * units, share),
            bf16(full, full), bf16(full, SHARES * units), bf16(full, SHARES * units),
            sems(2 * full // LONG + 2),
        ),
        50,
    )(spot, attended, stream, late, early, mod)
    result = vmem_call(closing_kernel, array(width, rows), [HERE])(spread(partial))
    return result.T.reshape(1, rows, width)


def solution(mesh):
    placed = (
        P(("dp", "frame"), None, "head"),
        P("dp", None),
        P("frame", None, "head"),
        P("head", "frame"),
        P("frame", None, "head"),
        P("head", "frame"),
        P("frame", "head"),
        P("head", "frame"),
    )
    return jax.shard_map(
        per_device,
        mesh=mesh,
        in_specs=placed,
        out_specs=P(("dp", "frame"), None, "head"),
        check_vma=False,
    )
```

```python
import math

import jax
import jax.numpy as jnp
from jax import lax
from jax.experimental import pallas as pl
from jax.experimental.pallas import tpu as pltpu
from jax.sharding import PartitionSpec as P

HEAD_DIM = 72
EPS = 1e-06
FACTOR = 1.0 / math.sqrt(HEAD_DIM)
LANES = 128
SHARES = 2
PLACE = 16
PARTS = LANES // PLACE
BLOCK = 144
STEP = 576
LONG = 1152
UNITS = 512
FEATURES = 432


def project(weight, hidden):
    return lax.dot_general(
        weight, hidden, (((0,), (0,)), ((), ())), preferred_element_type=jnp.float32
    )


def exchange(pieces):
    part = lax.broadcasted_iota(jnp.int32, pieces[0].shape, 1) // PLACE
    step = 1
    while step < PARTS:
        held = list(pieces)
        high = (part // step) % 2 == 1
        for i in range(PARTS):
            if i & step:
                continue
            low_piece, high_piece = pieces[i], pieces[i + step]
            held[i] = jnp.where(high, pltpu.roll(high_piece, step * PLACE, 1), low_piece)
            held[i + step] = jnp.where(high, high_piece, pltpu.roll(low_piece, LANES - step * PLACE, 1))
        pieces, step = held, 2 * step
    return pieces


def pack(block, out_ref, group):
    features, rows = block.shape
    if features < PARTS * group:
        block = jnp.concatenate([block, jnp.zeros((PARTS * group - features, rows), block.dtype)], 0)
    for tile in range(rows // LANES):
        cut = block[:, tile * LANES : (tile + 1) * LANES]
        pieces = [cut[at : at + group] for at in range(0, PARTS * group, group)]
        for spot, piece in enumerate(exchange(pieces)):
            out_ref[tile * PARTS + spot] = piece.astype(out_ref.dtype)


def unpack(in_ref, features):
    tiles = []
    for tile in range(in_ref.shape[0] // PARTS):
        held = [in_ref[tile * PARTS + spot].astype(jnp.float32) for spot in range(PARTS)]
        tiles.append(jnp.concatenate(exchange(held), 0)[:features])
    return jnp.concatenate(tiles, 1)


def norm_heads(mixed):
    features, rows = mixed.shape
    parts = mixed.reshape(features // HEAD_DIM, HEAD_DIM, rows)
    scale = lax.rsqrt(jnp.mean(parts * parts, axis=1, keepdims=True) + EPS)
    normed = (parts * scale).reshape(features, rows)
    pairs = 2 * features // 3
    return jnp.concatenate([normed[:pairs], mixed[pairs:]], 0)


def attend(mixed, same=None):
    third = mixed.shape[0] // 3
    outs = []
    for at in range(0, third, HEAD_DIM):
        query, key, value = (mixed[at + i * third : at + i * third + HEAD_DIM] for i in range(3))
        weights = jnp.exp(project(key, query) * FACTOR)
        if same is not None:
            weights = jnp.where(same, weights, 0.0)
        inverse = 1.0 / jnp.sum(weights, axis=0, keepdims=True)
        weights = (weights * inverse).astype(jnp.bfloat16)
        outs.append(jnp.dot(value, weights, preferred_element_type=jnp.float32))
    return jnp.concatenate(outs, 0)


def norm_rows(read, full, shift, scale, hidden_ref):
    steps = range(0, full, BLOCK)
    mean = sum(jnp.sum(read(at), axis=0, keepdims=True) for at in steps) / full
    spread = 0.0
    for at in steps:
        center = read(at) - mean
        spread += jnp.sum(center * center, axis=0, keepdims=True)
    inverse = lax.rsqrt(spread / full + EPS)
    for at in steps:
        spot = slice(at, at + BLOCK)
        normal = (read(at) - mean) * inverse
        hidden_ref[spot] = (normal * (1.0 + scale[spot]) + shift[spot]).astype(jnp.bfloat16)


def add_branch(weight, hidden, stream, gate, out_ref, whole_ref, step=STEP):
    for at in range(0, hidden.shape[0], step):
        branch = jnp.dot(weight(at), hidden, preferred_element_type=jnp.float32)
        for inner in range(0, step, BLOCK):
            spot = slice(at + inner, at + inner + BLOCK)
            gated = gate[spot] * branch[inner : inner + BLOCK]
            total = (stream(at + inner).astype(jnp.float32) + gated).astype(jnp.bfloat16)
            out_ref[spot] = total
            whole_ref[spot] = total.astype(jnp.float32)


def start_copies(pairs, sems):
    copies = [pltpu.make_async_copy(a, b, sems.at[i]) for i, (a, b) in enumerate(pairs)]
    for copy in copies:
        copy.start()
    return copies


def blocks(weight_ref, held, step=STEP):
    full, cols = held.shape
    spots = [pl.ds(at, step) for at in range(0, full, step)]
    return [(weight_ref.at[spot, pl.ds(0, cols)], held.at[spot]) for spot in spots]


def turned_copies_kernel(in_ref, out_ref):
    turned = in_ref[...].T
    for at in range(out_ref.shape[0]):
        out_ref[at] = turned


def side_by_side_kernel(*refs):
    out_ref, at = refs[-1], 0
    for ref in refs[:-1]:
        out_ref[:, at : at + ref.shape[1]] = ref[...]
        at += ref.shape[1]


def opening_kernel(own_ref, late_ref, mod_ref, rows_ref, mod_out_ref):
    rows, cols = own_ref.shape[1], late_ref.shape[1]
    for at in range(rows_ref.shape[0]):
        rows_ref[at, :, :rows] = own_ref[...]
        rows_ref[at, :, rows : rows + cols] = late_ref[...]
    mod_out_ref[...] = mod_ref[...].T


def late_weights_kernel(rows_ref, mlp_ref, others_ref, out_ref):
    depth, units = mlp_ref.shape[0], mlp_ref.shape[1] // 2
    turned = [rows_ref[at, :, :depth].T for at in range(rows_ref.shape[0])]
    pieces = turned + [mlp_ref[:, units:], others_ref[:, units:], mlp_ref[:, UNITS:units], others_ref[:, :units]]
    out_ref[...] = jnp.concatenate(pieces, 1)


def spatial_kernel(rows_ref, weight_ref, mod_ref, out_ref, hidden):
    full, rows = hidden.shape
    read = lambda at: rows_ref[at // BLOCK, :, :rows].astype(jnp.float32)
    norm_rows(read, full, mod_ref[:, 0:1], mod_ref[:, 1:2], hidden)
    mixed = norm_heads(project(weight_ref[...], hidden[...])).astype(jnp.bfloat16)
    block = attend(mixed).astype(out_ref.dtype)
    share = rows // SHARES
    for at in range(out_ref.shape[0]):
        first = at % SHARES * share
        out_ref[at] = block[:, first : first + share]


def spatial_end_kernel(
    spot_ref, gathered_ref, rows_ref, weight_ref, mod_ref, mixed_ref, stream_ref, whole, hidden, held, qkv, sems
):
    full, share = stream_ref.shape
    pairs = blocks(weight_ref, held) + [(weight_ref.at[:, pl.ds(full, qkv.shape[1])], qkv)]
    copies = start_copies(pairs, sems)
    mine = pl.ds(pl.multiple_of(spot_ref[1] * share, share), share)

    def weight(at):
        copies[at // STEP].wait()
        return held[at : at + STEP]

    add_branch(
        weight,
        gathered_ref[...].reshape(full, share),
        lambda at: rows_ref[at // BLOCK, :, mine],
        mod_ref[:, 2:3],
        stream_ref,
        whole,
    )
    norm_rows(lambda at: whole[at : at + BLOCK], full, mod_ref[:, 3:4], mod_ref[:, 4:5], hidden)
    copies[-1].wait()
    mixed = project(qkv[:, : SHARES * FEATURES], hidden[...])
    mixed = [norm_heads(mixed[at : at + FEATURES]) for at in range(0, SHARES * FEATURES, FEATURES)]
    pack(jnp.concatenate(mixed, 0), mixed_ref, mixed_ref.shape[1])


def temporal_kernel(moved_ref, out_ref):
    mixed = unpack(moved_ref, SHARES * FEATURES).astype(jnp.bfloat16)
    rows = mixed.shape[1]
    spot = lax.broadcasted_iota(jnp.int32, (rows, rows), 0) % PLACE
    spot_q = lax.broadcasted_iota(jnp.int32, (rows, rows), 1) % PLACE
    same = spot == spot_q
    outs = [attend(mixed[at : at + FEATURES], same) for at in range(0, SHARES * FEATURES, FEATURES)]
    pack(jnp.concatenate(outs, 0), out_ref, out_ref.shape[1])


def copies_kernel(spot_ref, moved_ref, out_ref):
    block = unpack(moved_ref, SHARES * BLOCK).astype(out_ref.dtype)
    own = pl.ds(pl.multiple_of(spot_ref[1] * BLOCK, BLOCK), BLOCK)
    other = pl.ds(pl.multiple_of((1 - spot_ref[1]) * BLOCK, BLOCK), BLOCK)
    for at in range(out_ref.shape[0]):
        out_ref[at, own, :] = block[:BLOCK]
        out_ref[at, other, :] = block[BLOCK:]


def mlp_kernel(
    spot_ref, gathered_ref, before_ref, weight_ref, early_ref, mod_ref, partial_ref, stream, whole, hidden,
    active, held, up, down, sems,
):
    full, rows = stream.shape
    units = active.shape[0]
    cuts = [(0, UNITS), (UNITS, units - UNITS)]
    pairs = blocks(weight_ref, held, LONG)
    pairs.append((early_ref.at[:, pl.ds(early_ref.shape[1] - UNITS, UNITS)], up.at[:, pl.ds(0, UNITS)]))
    rest = units - UNITS
    pairs.append((weight_ref.at[:, pl.ds(full + units, rest)], up.at[:, pl.ds(UNITS, rest)]))
    for at in range(0, full, LONG):
        rows_at = pl.ds(at, LONG)
        pairs.append((weight_ref.at[rows_at, pl.ds(full, units)], down.at[rows_at]))
    copies = start_copies(pairs, sems)
    first = full // LONG

    def weight(at):
        copies[at // LONG].wait()
        return held[at : at + LONG]

    add_branch(
        weight,
        gathered_ref[...].reshape(full, rows),
        lambda at: before_ref[at : at + BLOCK],
        mod_ref[:, 5:6],
        stream,
        whole,
        LONG,
    )
    norm_rows(lambda at: whole[at : at + BLOCK], full, mod_ref[:, 6:7], mod_ref[:, 7:8], hidden)
    for i, (at, count) in enumerate(cuts):
        copies[first + i].wait()
        raised = project(up[:, at : at + count], hidden[...])
        active[at : at + count] = jax.nn.gelu(raised, approximate=True).astype(jnp.bfloat16)
    for i, at in enumerate(range(0, full, LONG)):
        copies[first + len(cuts) + i].wait()
        lowered = jnp.dot(down[at : at + LONG], active[...], preferred_element_type=jnp.float32)
        for inner in range(0, LONG, BLOCK):
            spot = slice(at + inner, at + inner + BLOCK)
            place = (at + inner) // BLOCK
            carried = jnp.where(spot_ref[0] == place // SHARES, whole[spot], 0.0)
            gated = mod_ref[spot, 8:9] * lowered[inner : inner + BLOCK]
            partial_ref[place] = (carried + gated).astype(jnp.bfloat16)


def closing_kernel(partial_ref, out_ref):
    count = partial_ref.shape[0]
    for i in range(SHARES):
        share = sum(partial_ref[at].astype(jnp.float32) for at in range(i, count, SHARES))
        out_ref[:, i * share.shape[1] : (i + 1) * share.shape[1]] = share.astype(out_ref.dtype)


HERE = pl.BlockSpec(memory_space=pltpu.VMEM)
THERE = pl.BlockSpec(memory_space=pltpu.HBM)
SCALAR = pl.BlockSpec(memory_space=pltpu.SMEM)


def vmem_call(kernel, out_shape, in_specs, scratch=(), limit=32):
    return pl.pallas_call(
        kernel,
        out_shape=out_shape,
        in_specs=in_specs,
        scratch_shapes=list(scratch),
        compiler_params=pltpu.CompilerParams(vmem_limit_bytes=limit * 2**20),
    )


def per_device(
    latents, modulation, spatial_qkv, spatial_out, temporal_qkv, temporal_out, mlp_up, mlp_down
):
    rows, width = latents.shape[1], latents.shape[2]
    heads_n, frames_n = lax.axis_size("head"), lax.axis_size("frame")
    full = width * heads_n
    depth = spatial_qkv.shape[0]
    units = mlp_up.shape[1]
    lines = heads_n // SHARES
    share = rows // SHARES
    place = lax.axis_index("head").astype(jnp.int32)
    spot = jnp.stack([place // SHARES, place % SHARES])
    array = lambda *shape, dtype=jnp.bfloat16: jax.ShapeDtypeStruct(shape, dtype)
    bf16 = lambda *shape: pltpu.VMEM(shape, jnp.bfloat16)
    f32 = lambda *shape: pltpu.VMEM(shape, jnp.float32)
    sems = lambda count: pltpu.SemaphoreType.DMA((count,))
    spread = lambda copies: lax.all_to_all(copies, "head", 0, 0, tiled=True)
    swap = lambda chunks: lax.all_to_all(chunks, "frame", 0, 0, tiled=True)
    gather_frame = lambda packed: lax.all_gather(packed, "frame", axis=0, tiled=True)
    along_x = [[x * SHARES + y for x in range(lines)] for y in range(SHARES)]
    across_y = [(x * SHARES + y, x * SHARES + 1 - y) for x in range(lines) for y in range(SHARES)]
    wide_qkv = SHARES * 3 * width + -SHARES * 3 * width % LANES

    others_qkv = lax.ppermute(temporal_qkv, "head", across_y)
    out_copies = vmem_call(turned_copies_kernel, array(heads_n, depth, width), [HERE])(spatial_out)
    mlp = vmem_call(side_by_side_kernel, array(depth, 2 * units), [HERE] * 2)(mlp_up, mlp_down.T)
    row_copies, mod = vmem_call(
        opening_kernel,
        (
            array(heads_n, width, rows + LANES),
            array(full, modulation.shape[0], dtype=jnp.float32),
        ),
        [HERE] * 3,
    )(latents.reshape(rows, width).T, temporal_out, modulation)

    pieces = [
        spread(out_copies).transpose(1, 0, 2).reshape(depth, full),
        temporal_qkv.reshape(depth, -1),
        others_qkv.reshape(depth, -1),
        jnp.zeros((depth, -SHARES * 3 * width % LANES), jnp.bfloat16),
        mlp_up[:, :UNITS],
    ]
    early = gather_frame(jnp.concatenate(pieces, axis=1))
    stream = spread(row_copies)
    s_qkv = gather_frame(spatial_qkv.reshape(depth, -1))

    s_qkv, mlp = lax.optimization_barrier((s_qkv, mlp))
    others = lax.ppermute(mlp, "head", across_y)

    attended = vmem_call(
        spatial_kernel, array(heads_n, width, share), [HERE] * 3, (bf16(full, rows),)
    )(stream, s_qkv, mod)
    t_out, attended = lax.optimization_barrier((stream[:, :, rows:], attended))
    late = vmem_call(
        late_weights_kernel, array(depth, full + 2 * SHARES * units - UNITS), [HERE] * 3
    )(t_out, mlp, others)
    late = gather_frame(late)

    mixed, stream = vmem_call(
        spatial_end_kernel,
        (array(frames_n, 112, LANES), array(full, share)),
        [SCALAR, HERE, HERE, THERE, HERE],
        (
            f32(full, share), bf16(full, share), bf16(full, full), bf16(full, wide_qkv),
            sems(full // STEP + 1),
        ),
        46,
    )(spot, spread(attended), stream, early, mod)
    attended = vmem_call(temporal_kernel, array(frames_n, 48, LANES), [HERE])(swap(mixed))
    attended = vmem_call(copies_kernel, array(lines, SHARES * width, share), [SCALAR, HERE])(
        spot, swap(attended)
    )
    attended = lax.all_to_all(attended, "head", 0, 0, axis_index_groups=along_x, tiled=True)

    partial = vmem_call(
        mlp_kernel,
        array(heads_n, width, share),
        [SCALAR, HERE, HERE, THERE, THERE, HERE],
        (
            bf16(full, share), f32(full, share), bf16(full, share), bf16(SHARES * units, share),
            bf16(full, full), bf16(full, SHARES * units), bf16(full, SHARES * units),
            sems(2 * full // LONG + 2),
        ),
        50,
    )(spot, attended, stream, late, early, mod)
    result = vmem_call(closing_kernel, array(width, rows), [HERE])(spread(partial))
    return result.T.reshape(1, rows, width)


def solution(mesh):
    placed = (
        P(("dp", "frame"), None, "head"),
        P("dp", None),
        P("frame", None, "head"),
        P("head", "frame"),
        P("frame", None, "head"),
        P("head", "frame"),
        P("frame", "head"),
        P("head", "frame"),
    )
    return jax.shard_map(
        per_device,
        mesh=mesh,
        in_specs=placed,
        out_specs=P(("dp", "frame"), None, "head"),
        check_vma=False,
    )
```

```python
import math

import jax
import jax.numpy as jnp
from jax import lax
from jax.experimental import pallas as pl
from jax.experimental.pallas import tpu as pltpu
from jax.sharding import PartitionSpec as P

HEAD_DIM = 72
EPS = 1e-06
FACTOR = 1.0 / math.sqrt(HEAD_DIM)
LANES = 128
SHARES = 2
PLACE = 16
PARTS = LANES // PLACE
BLOCK = 144
STEP = 576
LONG = 1152
UNITS = 512
FEATURES = 432


def project(weight, hidden):
    return lax.dot_general(
        weight, hidden, (((0,), (0,)), ((), ())), preferred_element_type=jnp.float32
    )


def exchange(pieces):
    part = lax.broadcasted_iota(jnp.int32, pieces[0].shape, 1) // PLACE
    step = 1
    while step < PARTS:
        held = list(pieces)
        high = (part // step) % 2 == 1
        for i in range(PARTS):
            if i & step:
                continue
            low_piece, high_piece = pieces[i], pieces[i + step]
            held[i] = jnp.where(high, pltpu.roll(high_piece, step * PLACE, 1), low_piece)
            held[i + step] = jnp.where(high, high_piece, pltpu.roll(low_piece, LANES - step * PLACE, 1))
        pieces, step = held, 2 * step
    return pieces


def pack(block, out_ref, group):
    features, rows = block.shape
    if features < PARTS * group:
        block = jnp.concatenate([block, jnp.zeros((PARTS * group - features, rows), block.dtype)], 0)
    for tile in range(rows // LANES):
        cut = block[:, tile * LANES : (tile + 1) * LANES]
        pieces = [cut[at : at + group] for at in range(0, PARTS * group, group)]
        for spot, piece in enumerate(exchange(pieces)):
            out_ref[tile * PARTS + spot] = piece.astype(out_ref.dtype)


def unpack(in_ref, features):
    tiles = []
    for tile in range(in_ref.shape[0] // PARTS):
        held = [in_ref[tile * PARTS + spot].astype(jnp.float32) for spot in range(PARTS)]
        tiles.append(jnp.concatenate(exchange(held), 0)[:features])
    return jnp.concatenate(tiles, 1)


def norm_heads(mixed):
    features, rows = mixed.shape
    parts = mixed.reshape(features // HEAD_DIM, HEAD_DIM, rows)
    scale = lax.rsqrt(jnp.mean(parts * parts, axis=1, keepdims=True) + EPS)
    normed = (parts * scale).reshape(features, rows)
    pairs = 2 * features // 3
    return jnp.concatenate([normed[:pairs], mixed[pairs:]], 0)


def attend(mixed, same=None):
    third = mixed.shape[0] // 3
    outs = []
    for at in range(0, third, HEAD_DIM):
        query, key, value = (mixed[at + i * third : at + i * third + HEAD_DIM] for i in range(3))
        weights = jnp.exp(project(key, query) * FACTOR)
        if same is not None:
            weights = jnp.where(same, weights, 0.0)
        inverse = 1.0 / jnp.sum(weights, axis=0, keepdims=True)
        weights = (weights * inverse).astype(jnp.bfloat16)
        outs.append(jnp.dot(value, weights, preferred_element_type=jnp.float32))
    return jnp.concatenate(outs, 0)


def norm_rows(read, full, shift, scale, hidden_ref):
    steps = range(0, full, BLOCK)
    mean = sum(jnp.sum(read(at), axis=0, keepdims=True) for at in steps) / full
    spread = 0.0
    for at in steps:
        center = read(at) - mean
        spread += jnp.sum(center * center, axis=0, keepdims=True)
    inverse = lax.rsqrt(spread / full + EPS)
    for at in steps:
        spot = slice(at, at + BLOCK)
        normal = (read(at) - mean) * inverse
        hidden_ref[spot] = (normal * (1.0 + scale[spot]) + shift[spot]).astype(jnp.bfloat16)


def add_branch(weight, hidden, stream, gate, out_ref, whole_ref, step=STEP):
    for at in range(0, hidden.shape[0], step):
        branch = jnp.dot(weight(at), hidden, preferred_element_type=jnp.float32)
        for inner in range(0, step, BLOCK):
            spot = slice(at + inner, at + inner + BLOCK)
            gated = gate[spot] * branch[inner : inner + BLOCK]
            total = (stream(at + inner).astype(jnp.float32) + gated).astype(jnp.bfloat16)
            out_ref[spot] = total
            whole_ref[spot] = total.astype(jnp.float32)


def start_copies(pairs, sems):
    copies = [pltpu.make_async_copy(a, b, sems.at[i]) for i, (a, b) in enumerate(pairs)]
    for copy in copies:
        copy.start()
    return copies


def blocks(weight_ref, held, step=STEP):
    full, cols = held.shape
    spots = [pl.ds(at, step) for at in range(0, full, step)]
    return [(weight_ref.at[spot, pl.ds(0, cols)], held.at[spot]) for spot in spots]


def turned_copies_kernel(in_ref, out_ref):
    turned = in_ref[...].T
    for at in range(out_ref.shape[0]):
        out_ref[at] = turned


def side_by_side_kernel(*refs):
    out_ref, at = refs[-1], 0
    for ref in refs[:-1]:
        out_ref[:, at : at + ref.shape[1]] = ref[...]
        at += ref.shape[1]


def opening_kernel(own_ref, late_ref, mod_ref, rows_ref, mod_out_ref):
    rows, cols = own_ref.shape[1], late_ref.shape[1]
    for at in range(rows_ref.shape[0]):
        rows_ref[at, :, :rows] = own_ref[...]
        rows_ref[at, :, rows : rows + cols] = late_ref[...]
    mod_out_ref[...] = mod_ref[...].T


def late_weights_kernel(rows_ref, mlp_ref, others_ref, out_ref):
    depth, units = mlp_ref.shape[0], mlp_ref.shape[1] // 2
    turned = [rows_ref[at, :, :depth].T for at in range(rows_ref.shape[0])]
    pieces = turned + [mlp_ref[:, units:], others_ref[:, units:], mlp_ref[:, UNITS:units], others_ref[:, :units]]
    out_ref[...] = jnp.concatenate(pieces, 1)


def spatial_kernel(rows_ref, weight_ref, mod_ref, out_ref, hidden):
    full, rows = hidden.shape
    read = lambda at: rows_ref[at // BLOCK, :, :rows].astype(jnp.float32)
    norm_rows(read, full, mod_ref[:, 0:1], mod_ref[:, 1:2], hidden)
    mixed = norm_heads(project(weight_ref[...], hidden[...])).astype(jnp.bfloat16)
    block = attend(mixed).astype(out_ref.dtype)
    share = rows // SHARES
    for at in range(out_ref.shape[0]):
        first = at % SHARES * share
        out_ref[at] = block[:, first : first + share]


def spatial_end_kernel(
    spot_ref, gathered_ref, rows_ref, weight_ref, mod_ref, mixed_ref, stream_ref, whole, hidden, held, qkv, sems
):
    full, share = stream_ref.shape
    pairs = blocks(weight_ref, held) + [(weight_ref.at[:, pl.ds(full, qkv.shape[1])], qkv)]
    copies = start_copies(pairs, sems)
    mine = pl.ds(pl.multiple_of(spot_ref[1] * share, share), share)

    def weight(at):
        copies[at // STEP].wait()
        return held[at : at + STEP]

    add_branch(
        weight,
        gathered_ref[...].reshape(full, share),
        lambda at: rows_ref[at // BLOCK, :, mine],
        mod_ref[:, 2:3],
        stream_ref,
        whole,
    )
    norm_rows(lambda at: whole[at : at + BLOCK], full, mod_ref[:, 3:4], mod_ref[:, 4:5], hidden)
    copies[-1].wait()
    mixed = project(qkv[:, : SHARES * FEATURES], hidden[...])
    mixed = [norm_heads(mixed[at : at + FEATURES]) for at in range(0, SHARES * FEATURES, FEATURES)]
    pack(jnp.concatenate(mixed, 0), mixed_ref, mixed_ref.shape[1])


def temporal_kernel(moved_ref, out_ref):
    mixed = unpack(moved_ref, SHARES * FEATURES).astype(jnp.bfloat16)
    rows = mixed.shape[1]
    spot = lax.broadcasted_iota(jnp.int32, (rows, rows), 0) % PLACE
    spot_q = lax.broadcasted_iota(jnp.int32, (rows, rows), 1) % PLACE
    same = spot == spot_q
    outs = [attend(mixed[at : at + FEATURES], same) for at in range(0, SHARES * FEATURES, FEATURES)]
    pack(jnp.concatenate(outs, 0), out_ref, out_ref.shape[1])


def copies_kernel(spot_ref, moved_ref, out_ref):
    block = unpack(moved_ref, SHARES * BLOCK).astype(out_ref.dtype)
    own = pl.ds(pl.multiple_of(spot_ref[1] * BLOCK, BLOCK), BLOCK)
    other = pl.ds(pl.multiple_of((1 - spot_ref[1]) * BLOCK, BLOCK), BLOCK)
    for at in range(out_ref.shape[0]):
        out_ref[at, own, :] = block[:BLOCK]
        out_ref[at, other, :] = block[BLOCK:]


def mlp_kernel(
    spot_ref, gathered_ref, before_ref, weight_ref, early_ref, mod_ref, partial_ref, stream, whole, hidden,
    active, held, up, down, sems,
):
    full, rows = stream.shape
    units = active.shape[0]
    cuts = [(0, UNITS), (UNITS, units - UNITS)]
    pairs = blocks(weight_ref, held, LONG)
    pairs.append((early_ref.at[:, pl.ds(early_ref.shape[1] - UNITS, UNITS)], up.at[:, pl.ds(0, UNITS)]))
    rest = units - UNITS
    pairs.append((weight_ref.at[:, pl.ds(full + units, rest)], up.at[:, pl.ds(UNITS, rest)]))
    for at in range(0, full, LONG):
        rows_at = pl.ds(at, LONG)
        pairs.append((weight_ref.at[rows_at, pl.ds(full, units)], down.at[rows_at]))
    copies = start_copies(pairs, sems)
    first = full // LONG

    def weight(at):
        copies[at // LONG].wait()
        return held[at : at + LONG]

    add_branch(
        weight,
        gathered_ref[...].reshape(full, rows),
        lambda at: before_ref[at : at + BLOCK],
        mod_ref[:, 5:6],
        stream,
        whole,
        LONG,
    )
    norm_rows(lambda at: whole[at : at + BLOCK], full, mod_ref[:, 6:7], mod_ref[:, 7:8], hidden)
    for i, (at, count) in enumerate(cuts):
        copies[first + i].wait()
        raised = project(up[:, at : at + count], hidden[...])
        active[at : at + count] = jax.nn.gelu(raised, approximate=True).astype(jnp.bfloat16)
    for i, at in enumerate(range(0, full, LONG)):
        copies[first + len(cuts) + i].wait()
        lowered = jnp.dot(down[at : at + LONG], active[...], preferred_element_type=jnp.float32)
        for inner in range(0, LONG, BLOCK):
            spot = slice(at + inner, at + inner + BLOCK)
            place = (at + inner) // BLOCK
            carried = jnp.where(spot_ref[0] == place // SHARES, whole[spot], 0.0)
            gated = mod_ref[spot, 8:9] * lowered[inner : inner + BLOCK]
            partial_ref[place] = (carried + gated).astype(jnp.bfloat16)


def closing_kernel(partial_ref, out_ref):
    count = partial_ref.shape[0]
    for i in range(SHARES):
        share = sum(partial_ref[at].astype(jnp.float32) for at in range(i, count, SHARES))
        out_ref[:, i * share.shape[1] : (i + 1) * share.shape[1]] = share.astype(out_ref.dtype)


HERE = pl.BlockSpec(memory_space=pltpu.VMEM)
THERE = pl.BlockSpec(memory_space=pltpu.HBM)
SCALAR = pl.BlockSpec(memory_space=pltpu.SMEM)


def vmem_call(kernel, out_shape, in_specs, scratch=(), limit=32):
    return pl.pallas_call(
        kernel,
        out_shape=out_shape,
        in_specs=in_specs,
        scratch_shapes=list(scratch),
        compiler_params=pltpu.CompilerParams(vmem_limit_bytes=limit * 2**20),
    )


def per_device(
    latents, modulation, spatial_qkv, spatial_out, temporal_qkv, temporal_out, mlp_up, mlp_down
):
    rows, width = latents.shape[1], latents.shape[2]
    heads_n, frames_n = lax.axis_size("head"), lax.axis_size("frame")
    full = width * heads_n
    depth = spatial_qkv.shape[0]
    units = mlp_up.shape[1]
    lines = heads_n // SHARES
    share = rows // SHARES
    place = lax.axis_index("head").astype(jnp.int32)
    spot = jnp.stack([place // SHARES, place % SHARES])
    array = lambda *shape, dtype=jnp.bfloat16: jax.ShapeDtypeStruct(shape, dtype)
    bf16 = lambda *shape: pltpu.VMEM(shape, jnp.bfloat16)
    f32 = lambda *shape: pltpu.VMEM(shape, jnp.float32)
    sems = lambda count: pltpu.SemaphoreType.DMA((count,))
    spread = lambda copies: lax.all_to_all(copies, "head", 0, 0, tiled=True)
    swap = lambda chunks: lax.all_to_all(chunks, "frame", 0, 0, tiled=True)
    gather_frame = lambda packed: lax.all_gather(packed, "frame", axis=0, tiled=True)
    along_x = [[x * SHARES + y for x in range(lines)] for y in range(SHARES)]
    across_y = [(x * SHARES + y, x * SHARES + 1 - y) for x in range(lines) for y in range(SHARES)]
    wide_qkv = SHARES * 3 * width + -SHARES * 3 * width % LANES

    others_qkv = lax.ppermute(temporal_qkv, "head", across_y)
    out_copies = vmem_call(turned_copies_kernel, array(heads_n, depth, width), [HERE])(spatial_out)
    mlp = vmem_call(side_by_side_kernel, array(depth, 2 * units), [HERE] * 2)(mlp_up, mlp_down.T)
    others = lax.ppermute(mlp, "head", across_y)
    row_copies, mod = vmem_call(
        opening_kernel,
        (
            array(heads_n, width, rows + LANES),
            array(full, modulation.shape[0], dtype=jnp.float32),
        ),
        [HERE] * 3,
    )(latents.reshape(rows, width).T, temporal_out, modulation)

    pieces = [
        spread(out_copies).transpose(1, 0, 2).reshape(depth, full),
        temporal_qkv.reshape(depth, -1),
        others_qkv.reshape(depth, -1),
        jnp.zeros((depth, -SHARES * 3 * width % LANES), jnp.bfloat16),
        mlp_up[:, :UNITS],
    ]
    early = gather_frame(jnp.concatenate(pieces, axis=1))
    stream = spread(row_copies)
    s_qkv = gather_frame(spatial_qkv.reshape(depth, -1))

    attended = vmem_call(
        spatial_kernel, array(heads_n, width, share), [HERE] * 3, (bf16(full, rows),)
    )(stream, s_qkv, mod)
    t_out, attended = lax.optimization_barrier((stream[:, :, rows:], attended))
    late = vmem_call(
        late_weights_kernel, array(depth, full + 2 * SHARES * units - UNITS), [HERE] * 3
    )(t_out, mlp, others)
    late = gather_frame(late)

    mixed, stream = vmem_call(
        spatial_end_kernel,
        (array(frames_n, 112, LANES), array(full, share)),
        [SCALAR, HERE, HERE, THERE, HERE],
        (
            f32(full, share), bf16(full, share), bf16(full, full), bf16(full, wide_qkv),
            sems(full // STEP + 1),
        ),
        46,
    )(spot, spread(attended), stream, early, mod)
    attended = vmem_call(temporal_kernel, array(frames_n, 48, LANES), [HERE])(swap(mixed))
    attended = vmem_call(copies_kernel, array(lines, SHARES * width, share), [SCALAR, HERE])(
        spot, swap(attended)
    )
    attended = lax.all_to_all(attended, "head", 0, 0, axis_index_groups=along_x, tiled=True)

    partial = vmem_call(
        mlp_kernel,
        array(heads_n, width, share),
        [SCALAR, HERE, HERE, THERE, THERE, HERE],
        (
            bf16(full, share), f32(full, share), bf16(full, share), bf16(SHARES * units, share),
            bf16(full, full), bf16(full, SHARES * units), bf16(full, SHARES * units),
            sems(2 * full // LONG + 2),
        ),
        50,
    )(spot, attended, stream, late, early, mod)
    result = vmem_call(closing_kernel, array(width, rows), [HERE])(spread(partial))
    return result.T.reshape(1, rows, width)


def solution(mesh):
    placed = (
        P(("dp", "frame"), None, "head"),
        P("dp", None),
        P("frame", None, "head"),
        P("head", "frame"),
        P("frame", None, "head"),
        P("head", "frame"),
        P("frame", "head"),
        P("head", "frame"),
    )
    return jax.shard_map(
        per_device,
        mesh=mesh,
        in_specs=placed,
        out_specs=P(("dp", "frame"), None, "head"),
        check_vma=False,
    )
```
